512 devices in a mesh: tensor: 16 (over y_hi, z), shard: 16 (over x, y_lo), replica: 2 (over core).
Axes of the slice: x: 4, y: 8 (y_hi: 2, y_lo: 4; y = y_hi * 4 + y_lo), z: 8, core: 2. Of those that a mesh axis runs over, the one named last changes fastest.
Arguments:
- tokens: bfloat16 [4096, 4096], P(('tensor', 'shard', 'replica')), may hold values from -110 to 110
- grad_out: bfloat16 [4096, 4096], P(('tensor', 'shard', 'replica')), may hold values from -6 to 6
- norm_gain: float32 [4096], replicated, may hold values from 0.1 to 1.9
- norm_bias: float32 [4096], replicated, may hold values from -3 to 3
- up_weight: bfloat16 [4096, 8192], P('shard', 'tensor'), may hold values from -0.09375 to 0.09375
- up_bias: float32 [8192], P('tensor'), may hold values from -3 to 3
- down_weight: bfloat16 [8192, 4096], P('tensor', 'shard'), may hold values from -0.0625 to 0.0625
Outputs:
- input_grad: bfloat16 [4096, 4096], P(('tensor', 'shard', 'replica'))
- up_grad: float32 [4096, 8192], P(('shard', 'replica'), 'tensor')
- down_grad: float32 [8192, 4096], P('tensor', ('shard', 'replica'))
- up_bias_grad: float32 [8192], P('tensor')
- gain_grad: float32 [4096], replicated
- bias_grad: float32 [4096], replicated
The draws below stay inside these ranges and needn't reach their ends.
All inputs are finite; a program needn't handle non-finite values.
Results may differ from the reference program's by a relative error of at most 0.007.
Values may be sent and summed in bfloat16 or wider, within the bound.
A program may use at most 64 MiB of HBM per device.

```python
import math
import jax
import jax.numpy as jnp
from jax import lax

D = 4096
FF = 8192
TOKENS = 4096


def draw_tokens(key, part):
    key = jax.random.fold_in(key, 11)
    first, second, third = jax.random.split(key, 3)
    base = jnp.clip(jax.random.normal(first, (TOKENS, D), jnp.float32), -5.0, 5.0)
    row_scale = jnp.exp(jax.random.uniform(second, (TOKENS, 1), jnp.float32, 0.0, math.log(10.0)))
    col_scale = jnp.exp(jax.random.uniform(third, (1, D), jnp.float32, -0.7, 0.7))
    return (base * row_scale * col_scale).astype(jnp.bfloat16)


def shard_levels(stream_key, extent, pieces, smallest, largest):
    level = 1.0
    for dim, parts in pieces:
        draws = jax.random.uniform(jax.random.fold_in(jax.random.fold_in(stream_key, 6), dim), (parts,), jnp.float32, smallest / len(pieces), largest / len(pieces))
        level = level * jnp.repeat(jnp.exp(draws), extent[dim] // parts).reshape((-1,) + (1,) * (len(extent) - 1 - dim))
    return level


def noise(stream_key, extent, width, reach, cuts=(), dtype=jnp.bfloat16):
    loudness = shard_levels(stream_key, extent, cuts, -0.22, 0.18) if cuts else 1.0
    array = jax.random.normal(stream_key, extent, jnp.float32) * width * loudness
    return jnp.minimum(jnp.maximum(array, -reach), reach).astype(dtype)


def setup_inputs(seed: int = 0) -> dict:
    seeds = jax.random.split(jax.random.key(seed), 8)
    return {
        "tokens": draw_tokens(jax.random.fold_in(seeds[7], 71), 0),
        "grad_out": noise(seeds[1], (TOKENS, D), 1.0, 6.0, ((0, 512),)),
        "norm_gain": jnp.clip(1.0 + 0.18 * jax.random.normal(seeds[2], (D,), jnp.float32), 0.1, 1.9),
        "norm_bias": noise(seeds[3], (D,), 0.5, 3.0, (), jnp.float32),
        "up_weight": noise(seeds[4], (D, FF), D ** -0.5, 0.09375, ((0, 16), (1, 16))),
        "up_bias": noise(seeds[5], (FF,), 0.5, 3.0, ((0, 16),), jnp.float32),
        "down_weight": noise(seeds[6], (FF, D), FF ** -0.5, 0.0625, ((0, 16), (1, 16))),
    }


def dot_nt(left, right):
    return lax.dot_general(left, right, (((1,), (1,)), ((), ())), preferred_element_type=jnp.float32)

def dot_tn(left, right):
    return lax.dot_general(left, right, (((0,), (0,)), ((), ())), preferred_element_type=jnp.float32)

def normalize(values):
    widened = values.astype(jnp.float32)
    centred = widened - lax.optimization_barrier(jnp.mean(widened, axis=-1, keepdims=True))
    variance = lax.optimization_barrier(jnp.mean(centred * centred, axis=-1, keepdims=True))
    inverse_std = lax.rsqrt(variance + 1e-05)
    return (centred * inverse_std, inverse_std)

def norm_back(d_normed, standard, inverse_std, gain):
    scaled = d_normed * gain
    first = lax.optimization_barrier(jnp.mean(scaled, axis=-1, keepdims=True))
    second = lax.optimization_barrier(jnp.mean(scaled * standard, axis=-1, keepdims=True))
    return inverse_std * (scaled - first - standard * second)

def gelu_back(pre_act, upstream):
    result, pull_back = jax.vjp(jax.nn.gelu, pre_act)
    return pull_back(upstream)[0]

def reference(tokens, grad_out, norm_gain, norm_bias, up_weight, up_bias, down_weight):
    standard, inverse_std = normalize(tokens)
    normed = (standard * norm_gain + norm_bias).astype(jnp.bfloat16)
    pre_act = jnp.dot(normed, up_weight, preferred_element_type=jnp.float32) + up_bias
    act = jax.nn.gelu(pre_act).astype(jnp.bfloat16)
    d_act = dot_nt(grad_out, down_weight)
    d_hidden = gelu_back(pre_act, d_act).astype(jnp.bfloat16)
    down_grad = dot_tn(act, grad_out)
    up_grad = dot_tn(normed, d_hidden)
    up_bias_grad = lax.optimization_barrier(jnp.sum(d_hidden.astype(jnp.float32), axis=0))
    d_normed = dot_nt(d_hidden, up_weight)
    gain_grad = lax.optimization_barrier(jnp.sum(d_normed * standard, axis=0))
    bias_grad = lax.optimization_barrier(jnp.sum(d_normed, axis=0))
    d_in = norm_back(d_normed, standard, inverse_std, norm_gain)
    input_grad = (grad_out.astype(jnp.float32) + d_in).astype(jnp.bfloat16)
    return (input_grad, up_grad, down_grad, up_bias_grad, gain_grad, bias_grad)
```

```python
import functools
import jax
import jax.numpy as jnp
from jax import lax
from jax.experimental import pallas as pl
from jax.experimental.pallas import tpu as pltpu
from jax.sharding import PartitionSpec as P

MESH = pl.DeviceIdType.MESH
NX, NY, NZ = 4, 4, 8


class Links:
    def __init__(self, send, recv):
        self.send, self.recv, self.count, self.open = send, recv, 0, []

    def push(self, src, dst, landed, device):
        slot = self.count
        self.count += 1
        pltpu.make_async_remote_copy(
            src_ref=src, dst_ref=dst, send_sem=self.send.at[slot], recv_sem=self.recv.at[slot],
            device_id=device, device_id_type=MESH,
        ).start()
        arrival = pltpu.make_async_remote_copy(
            src_ref=src, dst_ref=landed, send_sem=self.send.at[slot], recv_sem=self.recv.at[slot],
            device_id=device, device_id_type=MESH,
        )
        self.open.append(arrival)
        return arrival

    def drain(self):
        for arrival in self.open:
            arrival.wait_send()
        self.open = []


def place():
    t, s, c = lax.axis_index("tensor"), lax.axis_index("shard"), lax.axis_index("replica")
    return t, s, c, s // NY, s % NY, t // NZ, t % NZ


def greet(devices):
    barrier = pltpu.get_barrier_semaphore()
    for device in devices:
        pl.semaphore_signal(barrier, inc=1, device_id=device, device_id_type=MESH)
    pl.semaphore_wait(barrier, len(devices))


def gather_kernel(rows_in, up_in, down_in, XG, WU, WD, raw, send, recv, local):
    t, s, c, x, yl, yh, z = place()
    sib = {"replica": 1 - c}
    xdev = lambda k: {"shard": ((x + k) % NX) * NY + yl}
    ydev = lambda k: {"shard": x * NY + (yl + k) % NY}
    zdev = lambda k: {"tensor": yh * NZ + (z + k) % NZ}
    opp = {"tensor": (1 - yh) * NZ + z}
    sof = lambda dx, dy: ((x + dx + NX) % NX) * NY + (yl + dy + NY) % NY
    tof = lambda dh, dz: ((yh + dh) % 2) * NZ + (z + dz + NZ) % NZ
    net = Links(send, recv)

    half = pl.multiple_of(c * 256, 256)
    own_up, own_down = up_in.at[:, pl.ds(half, 256)], down_in.at[pl.ds(half, 256), :]
    mine = [
        pltpu.make_async_copy(own_up, WU.at[s], local.at[0]),
        pltpu.make_async_copy(own_down, WD.at[s], local.at[1]),
        pltpu.make_async_copy(rows_in, raw.at[c], local.at[2]),
    ]
    for copy in mine:
        copy.start()
    greet([sib, xdev(1), xdev(3), ydev(1), ydev(2), ydev(3), zdev(1), zdev(7), opp])

    first = net.push(rows_in, raw.at[c], raw.at[1 - c], sib)
    ych, xin = {}, {}
    for k in (1, 2, 3):
        ych[k] = (
            net.push(own_up, WU.at[s], WU.at[sof(0, -k)], ydev(k)),
            net.push(own_down, WD.at[s], WD.at[sof(0, -k)], ydev(k)),
        )

    def xsend(j):
        here = sof(0, -j)
        xin[j] = (
            net.push(WU.at[here], WU.at[here], WU.at[sof(-1, -j)], xdev(1)),
            net.push(WU.at[here], WU.at[here], WU.at[sof(1, -j)], xdev(3)),
            net.push(WD.at[here], WD.at[here], WD.at[sof(-1, -j)], xdev(1)),
            net.push(WD.at[here], WD.at[here], WD.at[sof(1, -j)], xdev(3)),
        )

    far = {}

    def xforward(j):
        left, right = sof(-1, -j), sof(1, -j)
        for arrival in xin[j]:
            arrival.wait_recv()
        far[j] = (
            net.push(WU.at[right], WU.at[right], WU.at[sof(2, -j)], xdev(3)),
            net.push(WD.at[left], WD.at[left], WD.at[sof(2, -j)], xdev(1)),
        )

    twin = []

    def share(slot, landed):
        twin.append(net.push(XG.at[c, slot], XG.at[c, slot], XG.at[1 - c, landed], sib))

    mine[0].wait()
    mine[1].wait()
    xsend(0)
    mine[2].wait()
    first.wait_recv()
    for i in range(2):
        XG[i, t] = jnp.concatenate([raw[0, i], raw[1, i]], axis=0).astype(jnp.bfloat16)
    over = net.push(XG.at[c, t], XG.at[c, t], XG.at[c, tof(1, 0)], opp)

    ring = {}

    def zsend(q, k):
        a, b = tof(q, -k), tof(q, k)
        right = net.push(XG.at[c, a], XG.at[c, a], XG.at[c, tof(q, -k - 1)], zdev(1)) if k < 3 or q == 0 else None
        left = net.push(XG.at[c, b], XG.at[c, b], XG.at[c, tof(q, k + 1)], zdev(7)) if k < 3 or q == 1 else None
        ring[q, k] = (right, left)

    def zland(q, k):
        right, left = ring[q, k]
        if right is not None:
            right.wait_recv()
        if left is not None:
            left.wait_recv()
        if k < 3:
            zsend(q, k + 1)
        if right is not None:
            share(tof(q, -k - 1), tof(q, -k - 1))
        if left is not None:
            share(tof(q, k + 1), tof(q, k + 1))

    def yland(j):
        for arrival in ych[j]:
            arrival.wait_recv()
        xsend(j)

    zsend(0, 0)
    yland(1)
    over.wait_recv()
    zsend(1, 0)
    share(tof(1, 0), tof(1, 0))
    zland(0, 0)
    yland(3)
    zland(1, 0)
    xforward(0)
    zland(0, 1)
    yland(2)
    zland(1, 1)
    xforward(1)
    zland(0, 2)
    zland(1, 2)
    xforward(3)
    zland(0, 3)
    zland(1, 3)
    xforward(2)
    for j in (0, 1, 3, 2):
        for arrival in far[j]:
            arrival.wait_recv()
    for arrival in twin:
        arrival.wait_recv()
    net.drain()


def gather(rows, up_weight, down_weight):
    vmem, any_ = pl.BlockSpec(memory_space=pltpu.VMEM), pl.BlockSpec(memory_space=pl.ANY)
    bf = jnp.bfloat16
    return pl.pallas_call(
        gather_kernel,
        out_shape=(
            jax.ShapeDtypeStruct((2, 16, 16, 4096), bf),
            jax.ShapeDtypeStruct((16, 256, 256), bf),
            jax.ShapeDtypeStruct((16, 256, 256), bf),
        ),
        in_specs=[vmem, any_, any_],
        out_specs=(vmem, vmem, vmem),
        scratch_shapes=[
            pltpu.VMEM((2, 2, 8, 4096), jnp.float32),
            pltpu.SemaphoreType.DMA((80,)),
            pltpu.SemaphoreType.DMA((80,)),
            pltpu.SemaphoreType.DMA((3,)),
        ],
        compiler_params=pltpu.CompilerParams(
            collective_id=0, has_side_effects=True, vmem_limit_bytes=40 << 20
        ),
    )(rows, up_weight, down_weight)


def dot_nt(left, right):
    return lax.dot_general(
        left, right, (((1,), (1,)), ((), ())), preferred_element_type=jnp.float32
    )


def dot_tn(left, right):
    return lax.dot_general(
        left, right, (((0,), (0,)), ((), ())), preferred_element_type=jnp.float32
    )


def normalize(values):
    widened = values.astype(jnp.float32)
    centred = widened - jnp.mean(widened, axis=-1, keepdims=True)
    variance = jnp.mean(centred * centred, axis=-1, keepdims=True)
    inverse_std = lax.rsqrt(variance + 1e-05)
    return (centred * inverse_std, inverse_std)


def norm_back(d_normed, standard, inverse_std, gain):
    scaled = d_normed * gain
    first = jnp.mean(scaled, axis=-1, keepdims=True)
    second = jnp.mean(scaled * standard, axis=-1, keepdims=True)
    return inverse_std * (scaled - first - standard * second)


def gelu_back(pre_act, upstream):
    result, pull_back = jax.vjp(jax.nn.gelu, pre_act)
    return pull_back(upstream)[0]


def shards(tokens, grad_out, norm_gain, norm_bias, up_weight, up_bias, down_weight):
    standard, inverse_std = normalize(tokens)
    normed_local = (standard * norm_gain + norm_bias).astype(jnp.bfloat16)
    rows = jnp.stack([normed_local.astype(jnp.float32), grad_out.astype(jnp.float32)])
    XG, WU, WD = gather(rows, up_weight, down_weight)
    c = lax.axis_index("replica")
    normed, grads = XG[0].reshape(256, 4096), XG[1].reshape(256, 4096)
    up_full = WU.reshape(4096, 256)
    down_full = WD.transpose(1, 0, 2).reshape(256, 4096)
    bias = lax.dynamic_slice_in_dim(up_bias, c * 256, 256)
    d_act = dot_nt(grads, down_full)
    pre_act = jnp.dot(normed, up_full, preferred_element_type=jnp.float32) + bias
    act = jax.nn.gelu(pre_act).astype(jnp.bfloat16)
    d_hidden = gelu_back(pre_act, d_act).astype(jnp.bfloat16)
    hidden_part = jnp.sum(d_hidden.astype(jnp.float32), axis=0)
    part = dot_nt(d_hidden, up_full).reshape(16, 2, 8, 4096).transpose(1, 0, 2, 3)
    part = lax.psum_scatter(part, "replica", scatter_dimension=0, tiled=True)
    d_normed = lax.psum_scatter(part.reshape(128, 4096), "tensor", scatter_dimension=0, tiled=True)
    gain_grad, bias_grad = lax.psum(
        (jnp.sum(d_normed * standard, axis=0), jnp.sum(d_normed, axis=0)),
        ("tensor", "shard", "replica"),
    )
    up_bias_grad = lax.all_gather(lax.psum(hidden_part, "shard"), "replica", axis=0, tiled=True)
    d_in = norm_back(d_normed, standard, inverse_std, norm_gain)
    input_grad = (grad_out.astype(jnp.float32) + d_in).astype(jnp.bfloat16)
    up_part = lax.psum_scatter(dot_tn(normed, d_hidden), "shard", scatter_dimension=0, tiled=True)
    down_part = lax.psum_scatter(dot_tn(act, grads), "shard", scatter_dimension=1, tiled=True)
    up_grad = lax.all_to_all(up_part, "replica", split_axis=0, concat_axis=1, tiled=True)
    down_grad = lax.all_to_all(down_part, "replica", split_axis=1, concat_axis=0, tiled=True)
    return (input_grad, up_grad, down_grad, up_bias_grad, gain_grad, bias_grad)


def solution(mesh):
    return jax.shard_map(
        shards,
        mesh=mesh,
        in_specs=(
            P(("tensor", "shard", "replica"), None),
            P(("tensor", "shard", "replica"), None),
            P(),
            P(),
            P("shard", "tensor"),
            P("tensor"),
            P("tensor", "shard"),
        ),
        out_specs=(
            P(("tensor", "shard", "replica"), None),
            P(("shard", "replica"), "tensor"),
            P("tensor", ("shard", "replica")),
            P("tensor"),
            P(),
            P(),
        ),
        check_vma=False,
    )
```

```python
import functools
import jax
import jax.numpy as jnp
from jax import lax
from jax.experimental import pallas as pl
from jax.experimental.pallas import tpu as pltpu
from jax.sharding import PartitionSpec as P

MESH = pl.DeviceIdType.MESH
NX, NY, NZ = 4, 4, 8


class Links:
    def __init__(self, send, recv):
        self.send, self.recv, self.count, self.open = send, recv, 0, []

    def push(self, src, dst, landed, device):
        slot = self.count
        self.count += 1
        pltpu.make_async_remote_copy(
            src_ref=src, dst_ref=dst, send_sem=self.send.at[slot], recv_sem=self.recv.at[slot],
            device_id=device, device_id_type=MESH,
        ).start()
        arrival = pltpu.make_async_remote_copy(
            src_ref=src, dst_ref=landed, send_sem=self.send.at[slot], recv_sem=self.recv.at[slot],
            device_id=device, device_id_type=MESH,
        )
        self.open.append(arrival)
        return arrival

    def drain(self):
        for arrival in self.open:
            arrival.wait_send()
        self.open = []


def place():
    t, s, c = lax.axis_index("tensor"), lax.axis_index("shard"), lax.axis_index("replica")
    return t, s, c, s // NY, s % NY, t // NZ, t % NZ


def greet(devices):
    barrier = pltpu.get_barrier_semaphore()
    for device in devices:
        pl.semaphore_signal(barrier, inc=1, device_id=device, device_id_type=MESH)
    pl.semaphore_wait(barrier, len(devices))


def mm(left, right, dims):
    return lax.dot_general(left, right, (dims, ((), ())), preferred_element_type=jnp.float32)


def kernel(
    tok_in, grad_in, gain_in, nbias_in, up_in, ubias_in, down_in,
    dx_out, up_out, down_out, sums_out,
    XG, WU, WD, raw, std, stdh, inv, act_t, dh, dh_t, pre, dact,
    dxp, dxr, dxs, zr, zsum, hin, dn16, dn, gz, gh, gsum, gb, gy, gx,
    P, CH, F, CE, DR, Y, YR, keep, ut, local, send, recv,
):
    bf, f32 = jnp.bfloat16, jnp.float32
    t, s, c, x, yl, yh, z = place()
    sib = {"replica": 1 - c}
    xdev = lambda k: {"shard": ((x + k) % NX) * NY + yl}
    ydev = lambda k: {"shard": x * NY + (yl + k) % NY}
    zdev = lambda k: {"tensor": yh * NZ + (z + k) % NZ}
    opp = {"tensor": (1 - yh) * NZ + z}
    sof = lambda dx, dy: ((x + dx + NX) % NX) * NY + (yl + dy + NY) % NY
    tof = lambda dh, dz: ((yh + dh) % 2) * NZ + (z + dz + NZ) % NZ
    net = Links(send, recv)

    half = pl.multiple_of(c * 256, 256)
    own_up, own_down = up_in.at[:, pl.ds(half, 256)], down_in.at[pl.ds(half, 256), :]
    mine = [
        pltpu.make_async_copy(own_up, WU.at[s], local.at[0]),
        pltpu.make_async_copy(own_down, WD.at[s], local.at[1]),
    ]
    for copy in mine:
        copy.start()
    greet([sib, opp] + [xdev(k) for k in (1, 2, 3)] + [ydev(k) for k in (1, 2, 3)] + [zdev(k) for k in range(1, NZ)])

    ych, xin = {}, {}
    for k in (1, 2, 3):
        ych[k] = (
            net.push(own_up, WU.at[s], WU.at[sof(0, -k)], ydev(k)),
            net.push(own_down, WD.at[s], WD.at[sof(0, -k)], ydev(k)),
        )

    def xsend(j):
        here = sof(0, -j)
        xin[j] = (
            net.push(WU.at[here], WU.at[here], WU.at[sof(-1, -j)], xdev(1)),
            net.push(WU.at[here], WU.at[here], WU.at[sof(1, -j)], xdev(3)),
            net.push(WD.at[here], WD.at[here], WD.at[sof(-1, -j)], xdev(1)),
            net.push(WD.at[here], WD.at[here], WD.at[sof(1, -j)], xdev(3)),
        )

    far = {}

    def xforward(j):
        left, right = sof(-1, -j), sof(1, -j)
        for arrival in xin[j]:
            arrival.wait_recv()
        far[j] = (
            net.push(WU.at[right], WU.at[right], WU.at[sof(2, -j)], xdev(3)),
            net.push(WD.at[left], WD.at[left], WD.at[sof(2, -j)], xdev(1)),
        )

    twin = []

    def share(slot, landed):
        twin.append(net.push(XG.at[c, slot], XG.at[c, slot], XG.at[1 - c, landed], sib))

    mine[0].wait()
    mine[1].wait()
    xsend(0)
    wide = tok_in[...].astype(f32)
    centred = wide - jnp.mean(wide, axis=-1, keepdims=True)
    istd = lax.rsqrt(jnp.mean(centred * centred, axis=-1, keepdims=True) + 1e-05)
    inv[...] = jnp.broadcast_to(istd, inv.shape)
    std[...] = centred * istd
    raw[c, 0] = (std[...] * gain_in[...] + nbias_in[...]).astype(bf).astype(f32)
    raw[c, 1] = grad_in[...].astype(f32)
    first = net.push(raw.at[c], raw.at[c], raw.at[1 - c], sib)
    other_cols = pl.ds(pl.multiple_of((1 - c) * 2048, 2048), 2048)
    my_cols = pl.ds(pl.multiple_of(c * 2048, 2048), 2048)
    stdh[c] = std[:, my_cols]
    std_in = net.push(std.at[:, other_cols], stdh.at[c], stdh.at[1 - c], sib)
    first.wait_recv()
    for i in range(2):
        XG[i, t] = jnp.concatenate([raw[0, i], raw[1, i]], axis=0).astype(jnp.bfloat16)
    over = net.push(XG.at[c, t], XG.at[c, t], XG.at[c, tof(1, 0)], opp)

    ring = {}

    def zsend(q, k):
        a, b = tof(q, -k), tof(q, k)
        right = net.push(XG.at[c, a], XG.at[c, a], XG.at[c, tof(q, -k - 1)], zdev(1)) if k < 3 or q == 0 else None
        left = net.push(XG.at[c, b], XG.at[c, b], XG.at[c, tof(q, k + 1)], zdev(7)) if k < 3 or q == 1 else None
        ring[q, k] = (right, left)

    def zland(q, k):
        right, left = ring[q, k]
        if right is not None:
            right.wait_recv()
        if left is not None:
            left.wait_recv()
        if k < 3:
            zsend(q, k + 1)
        if right is not None:
            share(tof(q, -k - 1), tof(q, -k - 1))
        if left is not None:
            share(tof(q, k + 1), tof(q, k + 1))

    def yland(j):
        for arrival in ych[j]:
            arrival.wait_recv()
        xsend(j)

    zsend(0, 0)
    yland(1)
    over.wait_recv()
    zsend(1, 0)
    share(tof(1, 0), tof(1, 0))
    zland(0, 0)
    yland(3)
    zland(1, 0)
    xforward(0)
    zland(0, 1)
    yland(2)
    zland(1, 1)
    xforward(1)
    zland(0, 2)
    zland(1, 2)
    xforward(3)
    zland(0, 3)
    zland(1, 3)
    xforward(2)

    for arrival in twin:
        arrival.wait_recv()

    def forward(s1):
        cols = pl.ds(pl.multiple_of(s1 * 256, 256), 256)
        pre[...] += mm(XG[0, :, :, cols].reshape(256, 256), WU[s1], ((1,), (0,)))
        dact[...] += mm(XG[1, :, :, cols].reshape(256, 256), WD[s1], ((1,), (1,)))

    pre[...] = jnp.broadcast_to(ubias_in[pl.ds(c, 1), :], pre.shape)
    dact[...] = jnp.zeros_like(dact)

    @pl.loop(0, 16)
    def _(s1):
        @pl.when(s1 // NY != (x + 2) % NX)
        def _():
            forward(s1)

    for j in (0, 1, 3, 2):
        for arrival in far[j]:
            arrival.wait_recv()

    @pl.loop(0, 4)
    def _(y1):
        forward(((x + 2) % NX) * NY + y1)

    v = pre[...]
    root = 0.7978845608028654
    th = jnp.tanh(root * (v + 0.044715 * v * v * v))
    act_t[...] = jnp.transpose(0.5 * v * (1.0 + th)).astype(bf)
    slope = 0.5 * (1.0 + th) + 0.5 * v * (1.0 - th * th) * (root * (1.0 + 3 * 0.044715 * v * v))
    grad_pre = (dact[...] * slope).astype(bf)
    dh[...] = grad_pre
    wide_pre = grad_pre.astype(f32)
    dh_t[...] = jnp.transpose(wide_pre).astype(bf)
    gb[...] = jnp.zeros_like(gb)
    gb[8:9, 0:256] = jnp.sum(wide_pre, axis=0, keepdims=True)

    @pl.loop(0, 8)
    def _(i):
        dxp[i] = mm(dh[...], WU[(1 - c) * 8 + i], ((1,), (1,))).astype(bf)

    dx_in = net.push(dxp, dxr, dxr, sib)

    chain, direct, ends, ysums = {}, {}, {}, {}

    def partials(k):
        @pl.loop(0, 4)
        def _(i):
            s1 = i * NY + (yl + k) % NY
            cols = pl.ds(pl.multiple_of(s1 * 256, 256), 256)
            P[0, s1] = mm(dh_t[...], XG[0, :, :, cols].reshape(256, 256), ((1,), (0,))).astype(bf)
            P[1, s1] = mm(act_t[...], XG[1, :, :, cols].reshape(256, 256), ((1,), (0,))).astype(bf)

        chain[k] = (
            net.push(P.at[0, sof(2, k)], CH.at[0, k], CH.at[0, k], xdev(3)),
            net.push(P.at[1, sof(2, k)], CH.at[1, k], CH.at[1, k], xdev(1)),
        )
        direct[k] = (
            net.push(P.at[0, sof(1, k)], DR.at[0, k], DR.at[0, k], xdev(1)),
            net.push(P.at[1, sof(-1, k)], DR.at[1, k], DR.at[1, k], xdev(3)),
        )

    def pass_on(k):
        for u, (dx, device) in enumerate(((-1, xdev(3)), (1, xdev(1)))):
            chain[k][u].wait_recv()
            F[u, k] = (CH[u, k].astype(f32) + P[u, sof(dx, k)].astype(f32)).astype(bf)
            ends[u, k] = net.push(F.at[u, k], CE.at[u, k], CE.at[u, k], device)

    def finish_x(k):
        for u in range(2):
            direct[k][u].wait_recv()
            ends[u, k].wait_recv()
            total = P[u, sof(0, k)].astype(f32) + CE[u, k].astype(f32) + DR[u, k].astype(f32)
            if k == 0:
                keep[u] = total
            else:
                Y[u, k] = total.astype(bf)
                ysums[u, k] = net.push(Y.at[u, k], YR.at[u, k], YR.at[u, k], ydev(k))

    partials(2)
    dx_in.wait_recv()

    @pl.loop(0, 8)
    def _(i):
        total = mm(dh[...], WU[c * 8 + i], ((1,), (1,))) + dxr[i].astype(f32)
        dxs[:, :, pl.ds(pl.multiple_of(i * 256, 256), 256)] = total.astype(bf).reshape(16, 16, 256)

    zin = []
    for k in (4, 3, 5, 2, 6, 1, 7):
        for h in range(2):
            zin.append(net.push(dxs.at[h * NZ + (z + k) % NZ], zr.at[k, h], zr.at[k, h], zdev(k)))
    partials(1)
    partials(3)
    partials(0)
    pass_on(2)
    pass_on(1)
    finish_x(2)
    pass_on(3)

    for arrival in zin:
        arrival.wait_recv()

    def zadd(h):
        total = dxs[h * NZ + z].astype(f32)
        for k in range(1, NZ):
            total += zr[k, h].astype(f32)
        return total

    zsum[...] = zadd(1 - yh)
    over = net.push(zsum, hin, hin, opp)
    dn16[...] = zadd(yh)
    finish_x(1)
    pass_on(0)
    over.wait_recv()
    dn16[...] += hin[...]
    rows_out = net.push(
        dn16.at[pl.ds(pl.multiple_of((1 - c) * 8, 8), 8), :], dn.at[c], dn.at[1 - c], sib
    )
    dn[c] = dn16[pl.ds(pl.multiple_of(c * 8, 8), 8), :]
    std_in.wait_recv()
    shared = jnp.concatenate([stdh[0], stdh[1]], axis=0)
    gsum_row = jnp.sum(dn16[...] * shared, axis=0, keepdims=True)
    bsum_row = jnp.sum(dn16[...], axis=0, keepdims=True)
    for i in range(4):
        gsum[i : i + 1, :] = gsum_row[:, i * 512 : (i + 1) * 512]
        gsum[4 + i : 5 + i, :] = bsum_row[:, i * 512 : (i + 1) * 512]
    zg = [net.push(gsum, gz.at[k], gz.at[k], zdev(k)) for k in range(1, NZ)]
    finish_x(3)
    rows_out.wait_recv()
    d_normed = jnp.concatenate([dn[0], dn[1]], axis=1)
    scaled = d_normed * gain_in[...]
    mean1 = jnp.mean(scaled, axis=-1, keepdims=True)
    mean2 = jnp.mean(scaled * std[...], axis=-1, keepdims=True)
    d_in = inv[:, 0:1] * (scaled - mean1 - std[...] * mean2)
    dx_out[...] = (grad_in[...].astype(f32) + d_in).astype(bf)
    total = gsum[...]
    for k, arrival in enumerate(zg, 1):
        arrival.wait_recv()
        total += gz[k]
    gb[0:8, :] = total
    hg = net.push(gb.at[0:8, :], gh, gh, opp)
    finish_x(0)
    hg.wait_recv()
    gy[0, 8:16, :] = gb[8:16, :]
    gy[0, 0:8, :] = gb[0:8, :] + gh[...]
    yg = [net.push(gy.at[0], gy.at[k], gy.at[k], ydev(k)) for k in (1, 2, 3)]
    for arrival in yg:
        arrival.wait_recv()
    gx[0] = gy[0] + gy[1] + gy[2] + gy[3]
    xg = [net.push(gx.at[0], gx.at[k], gx.at[k], xdev(k)) for k in (1, 2, 3)]
    for u in range(2):
        total = keep[u]
        for k in (1, 2, 3):
            ysums[u, k].wait_recv()
            total += YR[u, k].astype(f32)
        if u == 0:
            total = jnp.transpose(total)
        ut[u] = total
    my_half, its_half = (pl.ds(pl.multiple_of(h * 128, 128), 128) for h in (c, 1 - c))
    my_hid, its_hid = (pl.ds(pl.multiple_of(h * 256, 256), 256) for h in (c, 1 - c))
    last = [
        net.push(ut.at[0, its_half, :], up_out.at[:, my_hid], up_out.at[:, its_hid], sib),
        net.push(ut.at[1, :, its_half], down_out.at[my_hid, :], down_out.at[its_hid, :], sib),
    ]
    mine = [
        pltpu.make_async_copy(ut.at[0, my_half, :], up_out.at[:, my_hid], local.at[0]),
        pltpu.make_async_copy(ut.at[1, :, my_half], down_out.at[my_hid, :], local.at[1]),
    ]
    for copy in mine:
        copy.start()
    for arrival in xg:
        arrival.wait_recv()
    sums_out[c] = gx[0] + gx[1] + gx[2] + gx[3]
    last.append(net.push(sums_out.at[c], sums_out.at[c], sums_out.at[1 - c], sib))
    for arrival in last:
        arrival.wait_recv()
    for copy in mine:
        copy.wait()
    net.drain()


def shards(tokens, grad_out, norm_gain, norm_bias, up_weight, up_bias, down_weight):
    vmem, any_ = pl.BlockSpec(memory_space=pltpu.VMEM), pl.BlockSpec(memory_space=pl.ANY)
    bf, f32 = jnp.bfloat16, jnp.float32
    shape, room = jax.ShapeDtypeStruct, pltpu.VMEM
    input_grad, up_grad, down_grad, sums = pl.pallas_call(
        kernel,
        out_shape=(
            shape((8, 4096), bf), shape((128, 512), f32), shape((512, 128), f32), shape((2, 16, 512), f32),
        ),
        in_specs=[vmem, vmem, vmem, vmem, any_, vmem, any_],
        out_specs=(vmem, vmem, vmem, vmem),
        scratch_shapes=[
            room((2, 16, 16, 4096), bf),
            room((16, 256, 256), bf),
            room((16, 256, 256), bf),
            room((2, 2, 8, 4096), f32),
            room((8, 4096), f32),
            room((2, 8, 2048), f32),
            room((8, 128), f32),
            room((256, 256), bf),
            room((256, 256), bf),
            room((256, 256), bf),
            room((256, 256), f32),
            room((256, 256), f32),
            room((8, 256, 256), bf),
            room((8, 256, 256), bf),
            room((16, 16, 2048), bf),
            room((8, 2, 16, 2048), bf),
            room((16, 2048), f32),
            room((16, 2048), f32),
            room((16, 2048), f32),
            room((2, 8, 2048), f32),
            room((8, 8, 512), f32),
            room((8, 512), f32),
            room((8, 512), f32),
            room((16, 512), f32),
            room((4, 16, 512), f32),
            room((4, 16, 512), f32),
            room((2, 16, 256, 256), bf),
            room((2, 4, 256, 256), bf),
            room((2, 4, 256, 256), bf),
            room((2, 4, 256, 256), bf),
            room((2, 4, 256, 256), bf),
            room((2, 4, 256, 256), bf),
            room((2, 4, 256, 256), bf),
            room((2, 256, 256), f32),
            room((2, 256, 256), f32),
            pltpu.SemaphoreType.DMA((2,)),
            pltpu.SemaphoreType.DMA((160,)),
            pltpu.SemaphoreType.DMA((160,)),
        ],
        compiler_params=pltpu.CompilerParams(
            collective_id=0, has_side_effects=True, vmem_limit_bytes=50 << 20
        ),
    )(
        tokens, grad_out, norm_gain.reshape(1, 4096), norm_bias.reshape(1, 4096),
        up_weight, up_bias.reshape(2, 256), down_weight,
    )
    return (
        input_grad, up_grad, down_grad, sums[:, 8, :256].reshape(512),
        sums[:, 0:4].reshape(4096), sums[:, 4:8].reshape(4096),
    )


def solution(mesh):
    return jax.shard_map(
        shards,
        mesh=mesh,
        in_specs=(
            P(("tensor", "shard", "replica"), None),
            P(("tensor", "shard", "replica"), None),
            P(),
            P(),
            P("shard", "tensor"),
            P("tensor"),
            P("tensor", "shard"),
        ),
        out_specs=(
            P(("tensor", "shard", "replica"), None),
            P(("shard", "replica"), "tensor"),
            P("tensor", ("shard", "replica")),
            P("tensor"),
            P(),
            P(),
        ),
        check_vma=False,
    )
```

```python
import functools
import jax
import jax.numpy as jnp
from jax import lax
from jax.experimental import pallas as pl
from jax.experimental.pallas import tpu as pltpu
from jax.sharding import PartitionSpec as P

MESH = pl.DeviceIdType.MESH
NX, NY, NZ = 4, 4, 8


OFF = set()


def when(cond, body):
    if cond is None:
        body()
    else:
        pl.when(cond)(body)


class Nul:
    cond = None

    def wait_recv(self):
        pass

    def wait_send(self):
        pass


class Arrival:
    def __init__(self, copy, cond):
        self.copy, self.cond = copy, cond

    def wait_recv(self):
        when(self.cond, self.copy.wait_recv)

    def wait_send(self):
        when(self.cond, self.copy.wait_send)


class Links:
    def __init__(self, send, recv):
        self.send, self.recv, self.count, self.open = send, recv, 0, []

    def push(self, src, dst, landed, device, go=None, come=None):
        root = id(getattr(src, "ref", src))
        if self.groups.get(root, "D") in OFF:
            return Nul()
        slot = self.count
        self.count += 1
        pair = dict(
            send_sem=self.send.at[slot], recv_sem=self.recv.at[slot], device_id=device, device_id_type=MESH
        )
        when(go, pltpu.make_async_remote_copy(src_ref=src, dst_ref=dst, **pair).start)
        arrival = pltpu.make_async_remote_copy(src_ref=src, dst_ref=landed, **pair)
        self.open.append(Arrival(arrival, go))
        return Arrival(arrival, come)

    def drain(self):
        for arrival in self.open:
            arrival.wait_send()
        self.open = []


def place():
    t, s, c = lax.axis_index("tensor"), lax.axis_index("shard"), lax.axis_index("replica")
    return t, s, c, s // NY, s % NY, t // NZ, t % NZ


def greet(devices):
    barrier = pltpu.get_barrier_semaphore()
    for device in devices:
        pl.semaphore_signal(barrier, inc=1, device_id=device, device_id_type=MESH)
    pl.semaphore_wait(barrier, len(devices))


def mm(left, right, dims):
    return lax.dot_general(left, right, (dims, ((), ())), preferred_element_type=jnp.float32)


def kernel(
    tok_in, grad_in, gain_hbm, nbias_hbm, up_in, ubias_hbm, down_in,
    dx_out, up_out, down_out, sums_out,
    XG, XN, WU, WD, gain, nbias, ubias, raw, std, inv, mu, iv, act_t, dh, dh_t, pre, dact,
    dxp, dxr, dxs, zr, zsum, hin, dn16, dn, gz, gh, gsum, gb, gy, gx,
    P, CH, F, CE, DR, Y, YR, keep, ut, local, send, recv,
):
    bf, f32 = jnp.bfloat16, jnp.float32
    t, s, c, x, yl, yh, z = place()
    sib = {"replica": 1 - c}
    xdev = lambda k: {"shard": ((x + k) % NX) * NY + yl}
    ydev = lambda k: {"shard": x * NY + (yl + k) % NY}
    zdev = lambda k: {"tensor": yh * NZ + (z + k) % NZ}
    opp = {"tensor": (1 - yh) * NZ + z}
    sof = lambda dx, dy: ((x + dx + NX) % NX) * NY + (yl + dy + NY) % NY
    tof = lambda dh, dz: ((yh + dh) % 2) * NZ + (z + dz + NZ) % NZ
    net = Links(send, recv)
    root_of = lambda ref: id(getattr(ref, "ref", ref))
    net.groups = {root_of(r): g for g, rs in {"W": (up_in, down_in, WU, WD), "Z": (XG, raw), "X": (P, F, Y, ut)}.items() for r in rs}

    half = pl.multiple_of(c * 256, 256)
    own_up, own_down = up_in.at[:, pl.ds(half, 256)], down_in.at[pl.ds(half, 256), :]
    mine = [
        pltpu.make_async_copy(own_up, WU.at[s], local.at[0]),
        pltpu.make_async_copy(own_down, WD.at[s], local.at[1]),
        pltpu.make_async_copy(gain_hbm, gain, local.at[2]),
        pltpu.make_async_copy(nbias_hbm, nbias, local.at[3]),
        pltpu.make_async_copy(ubias_hbm, ubias, local.at[4]),
    ]
    for copy in mine:
        copy.start()
    raw[c, 0] = tok_in[...].astype(f32)
    raw[c, 1] = grad_in[...].astype(f32)
    greet([sib, opp] + [xdev(k) for k in (1, 2, 3)] + [ydev(k) for k in (1, 2, 3)] + [zdev(k) for k in range(1, NZ)])
    first = net.push(raw.at[c], raw.at[c], raw.at[1 - c], sib)
    mine[0].wait()
    mine[1].wait()

    has_left, has_right = yl > 0, yl < NY - 1
    line, xin, far = {}, {}, {}

    def there(side, k):
        return yl - 1 - k >= 0 if side < 0 else yl + 1 + k <= NY - 1

    def along(side, k):
        here, landed = sof(0, side * k), sof(0, side * (k + 1))
        if side < 0:
            go = has_right if k == 0 else jnp.logical_and(has_right, yl - k >= 0)
        else:
            go = has_left if k == 0 else jnp.logical_and(has_left, yl + k <= NY - 1)
        line[side, k] = [
            net.push(w.at[here], w.at[here], w.at[landed], ydev(1 if side < 0 else 3), go, there(side, k))
            for w in (WU, WD)
        ]

    def xsend(name, dy, cond):
        here, left, right = sof(0, dy), sof(-1, dy), sof(1, dy)
        xin[name] = [
            net.push(WU.at[here], WU.at[here], WU.at[right], xdev(3), cond, cond),
            net.push(WD.at[here], WD.at[here], WD.at[left], xdev(1), cond, cond),
            net.push(WU.at[here], WU.at[here], WU.at[left], xdev(1), cond, cond),
            net.push(WD.at[here], WD.at[here], WD.at[right], xdev(3), cond, cond),
        ]

    def xforward(name, dy, cond):
        left, right, opposite = sof(-1, dy), sof(1, dy), sof(2, dy)
        xin[name][0].wait_recv()
        one = net.push(WU.at[right], WU.at[right], WU.at[opposite], xdev(3), cond, cond)
        xin[name][1].wait_recv()
        two = net.push(WD.at[left], WD.at[left], WD.at[opposite], xdev(1), cond, cond)
        xin[name][2].wait_recv()
        xin[name][3].wait_recv()
        far[name] = (one, two)

    def yland(k):
        for side in (-1, 1):
            for arrival in line[side, k]:
                arrival.wait_recv()
            if k < 2:
                along(side, k + 1)
            xsend((side, k), side * (k + 1), there(side, k))

    def pass_x(k):
        for side in (-1, 1):
            xforward((side, k), side * (k + 1), there(side, k))

    along(-1, 0)
    along(1, 0)
    xsend("own", 0, None)

    twin, ring = {}, {}

    def share(name, slot):
        twin.setdefault(name, []).append(net.push(XG.at[c, slot], XG.at[c, slot], XG.at[1 - c, slot], sib))

    def zsend(q, k):
        a, b = tof(q, -k), tof(q, k)
        right = net.push(XG.at[c, a], XG.at[c, a], XG.at[c, tof(q, -k - 1)], zdev(1)) if k < 3 or q == 0 else None
        left = net.push(XG.at[c, b], XG.at[c, b], XG.at[c, tof(q, k + 1)], zdev(7)) if k < 3 or q == 1 else None
        ring[q, k] = (right, left)

    def zland(q, k):
        right, left = ring[q, k]
        if right is not None:
            right.wait_recv()
        if left is not None:
            left.wait_recv()
        if k < 3:
            zsend(q, k + 1)
        if right is not None:
            share(k, tof(q, -k - 1))
        if left is not None:
            share(k, tof(q, k + 1))

    def normalize(slot):
        wide = XG[0, slot].astype(f32)
        mean = jnp.mean(wide, axis=-1, keepdims=True)
        centred = wide - mean
        istd = lax.rsqrt(jnp.mean(centred * centred, axis=-1, keepdims=True) + 1e-05)
        XN[slot] = (centred * istd * gain[...] + nbias[...]).astype(bf)
        mu[slot] = jnp.broadcast_to(mean, (16, 128))
        iv[slot] = jnp.broadcast_to(istd, (16, 128))

    def settle(k):
        for arrival in twin[k]:
            arrival.wait_recv()
        if k == "y":
            normalize(tof(1, 0))
        elif k < 3:

            @pl.loop(0, 4)
            def _(i):
                normalize(((yh + i // 2) % 2) * NZ + (z + (2 * (i % 2) - 1) * (k + 1) + NZ) % NZ)
        else:

            @pl.loop(0, 2)
            def _(i):
                normalize(((yh + i) % 2) * NZ + (z + 4) % NZ)

    first.wait_recv()
    for i in range(2):
        XG[i, t] = jnp.concatenate([raw[0, i], raw[1, i]], axis=0).astype(bf)
    over = net.push(XG.at[c, t], XG.at[c, t], XG.at[c, tof(1, 0)], opp)
    zsend(0, 0)
    for copy in mine[2:]:
        copy.wait()
    normalize(t)
    yland(0)
    over.wait_recv()
    zsend(1, 0)
    share("y", tof(1, 0))
    zland(0, 0)
    xforward("own", 0, None)
    zland(1, 0)
    yland(1)
    settle("y")
    zland(0, 1)
    pass_x(0)
    zland(1, 1)
    yland(2)
    settle(0)
    zland(0, 2)
    zland(1, 2)
    settle(1)
    pass_x(1)
    zland(0, 3)
    zland(1, 3)
    settle(2)
    wide = raw[c, 0]
    centred = wide - jnp.mean(wide, axis=-1, keepdims=True)
    istd = lax.rsqrt(jnp.mean(centred * centred, axis=-1, keepdims=True) + 1e-05)
    inv[...] = jnp.broadcast_to(istd, inv.shape)
    std[...] = centred * istd
    settle(3)

    def forward(s1):
        cols = pl.ds(pl.multiple_of(s1 * 256, 256), 256)
        pre[...] += mm(XN[:, :, cols].reshape(256, 256), WU[s1], ((1,), (0,)))
        dact[...] += mm(XG[1, :, :, cols].reshape(256, 256), WD[s1], ((1,), (1,)))

    pre[...] = jnp.broadcast_to(ubias[:, pl.ds(half, 256)], pre.shape)
    dact[...] = jnp.zeros_like(dact)
    remote = lambda y1: jnp.abs(y1 - yl) == 3
    near = lambda i, y1: ((x + i + i // 2) % NX) * NY + y1

    @pl.loop(0, 12)
    def _(i):
        @pl.when(jnp.logical_not(remote(i // 3)))
        def _():
            forward(near(i % 3, i // 3))

    pass_x(2)
    for name in ("own", (-1, 0), (1, 0), (-1, 1), (1, 1)):
        for arrival in far[name]:
            arrival.wait_recv()

    @pl.loop(0, 4)
    def _(y1):
        @pl.when(jnp.logical_not(remote(y1)))
        def _():
            forward(((x + 2) % NX) * NY + y1)

    ends_line = jnp.logical_or(yl == 0, yl == 3)

    @pl.when(ends_line)
    def _():
        @pl.loop(0, 3)
        def _(i):
            forward(near(i, 3 - yl))

    for name in ((-1, 2), (1, 2)):
        for arrival in far[name]:
            arrival.wait_recv()

    @pl.when(ends_line)
    def _():
        forward(((x + 2) % NX) * NY + 3 - yl)

    v = pre[...]
    root = 0.7978845608028654
    th = jnp.tanh(root * (v + 0.044715 * v * v * v))
    slope = 0.5 * (1.0 + th) + 0.5 * v * (1.0 - th * th) * (root * (1.0 + 3 * 0.044715 * v * v))
    grad_pre = (dact[...] * slope).astype(bf)
    dh[...] = grad_pre

    @pl.loop(0, 8)
    def _(i):
        dxp[i] = mm(dh[...], WU[(1 - c) * 8 + i], ((1,), (1,))).astype(bf)

    dx_in = net.push(dxp, dxr, dxr, sib)
    wide_pre = grad_pre.astype(f32)
    dh_t[...] = jnp.transpose(wide_pre).astype(bf)
    act_t[...] = jnp.transpose(0.5 * v * (1.0 + th)).astype(bf)
    gb[16:24, :] = jnp.broadcast_to(jnp.sum(wide_pre, axis=0, keepdims=True), (8, 256))

    chain, direct, ends, ysums = {}, {}, {}, {}

    def partials(k):
        @pl.loop(0, 4)
        def _(i):
            s1 = i * NY + (yl + k) % NY
            cols = pl.ds(pl.multiple_of(s1 * 256, 256), 256)
            P[0, s1] = mm(dh_t[...], XN[:, :, cols].reshape(256, 256), ((1,), (0,))).astype(bf)
            P[1, s1] = mm(act_t[...], XG[1, :, :, cols].reshape(256, 256), ((1,), (0,))).astype(bf)

        chain[k] = (
            net.push(P.at[0, sof(2, k)], CH.at[0, k], CH.at[0, k], xdev(3)),
            net.push(P.at[1, sof(2, k)], CH.at[1, k], CH.at[1, k], xdev(1)),
        )
        direct[k] = (
            net.push(P.at[0, sof(1, k)], DR.at[0, k], DR.at[0, k], xdev(1)),
            net.push(P.at[1, sof(-1, k)], DR.at[1, k], DR.at[1, k], xdev(3)),
        )

    def pass_on(k):
        for u, (dx, device) in enumerate(((-1, xdev(3)), (1, xdev(1)))):
            chain[k][u].wait_recv()
            F[u, k] = (CH[u, k].astype(f32) + P[u, sof(dx, k)].astype(f32)).astype(bf)
            ends[u, k] = net.push(F.at[u, k], CE.at[u, k], CE.at[u, k], device)

    def finish_x(k):
        for u in range(2):
            direct[k][u].wait_recv()
            ends[u, k].wait_recv()
            total = P[u, sof(0, k)].astype(f32) + CE[u, k].astype(f32) + DR[u, k].astype(f32)
            if k == 0:
                keep[u] = total
            else:
                Y[u, k] = total.astype(bf)
                ysums[u, k] = net.push(Y.at[u, k], YR.at[u, k], YR.at[u, k], ydev(k))

    partials(2)
    dx_in.wait_recv()

    @pl.loop(0, 8)
    def _(i):
        total = mm(dh[...], WU[c * 8 + i], ((1,), (1,))) + dxr[i].astype(f32)
        dxs[:, :, pl.ds(pl.multiple_of(i * 256, 256), 256)] = total.astype(bf).reshape(16, 16, 256)
        cols = pl.ds(pl.multiple_of((c * 8 + i) * 256, 256), 256)
        tok = XG[0, :, :, cols].reshape(256, 256).astype(f32)
        standard = (tok - mu[...].reshape(256, 128)[:, 0:1]) * iv[...].reshape(256, 128)[:, 0:1]
        gsum[pl.ds(i, 1), :] = jnp.sum(total * standard, axis=0, keepdims=True)
        gsum[pl.ds(8 + i, 1), :] = jnp.sum(total, axis=0, keepdims=True)

    zg = [net.push(gsum, gz.at[k], gz.at[k], zdev(k)) for k in range(1, NZ)]
    zin = []
    for k in (4, 3, 5, 2, 6, 1, 7):
        for h in range(2):
            zin.append(net.push(dxs.at[h * NZ + (z + k) % NZ], zr.at[k, h], zr.at[k, h], zdev(k)))
    partials(1)
    pass_on(2)
    partials(3)
    pass_on(1)
    finish_x(2)
    partials(0)
    total = gsum[...]
    for k, arrival in enumerate(zg, 1):
        arrival.wait_recv()
        total += gz[k]
    gb[0:16, :] = total
    hg = net.push(gb.at[0:16, :], gh, gh, opp)
    pass_on(3)
    finish_x(1)
    hg.wait_recv()
    gy[0, 16:24, :] = gb[16:24, :]
    gy[0, 0:16, :] = gb[0:16, :] + gh[...]
    yg = [net.push(gy.at[0], gy.at[k], gy.at[k], ydev(k)) for k in (1, 2, 3)]

    for arrival in zin:
        arrival.wait_recv()

    def zadd(h):
        total = dxs[h * NZ + z].astype(f32)
        for k in range(1, NZ):
            total += zr[k, h].astype(f32)
        return total

    zsum[...] = zadd(1 - yh)
    over = net.push(zsum, hin, hin, opp)
    dn16[...] = zadd(yh)
    pass_on(0)
    finish_x(3)
    for arrival in yg:
        arrival.wait_recv()
    gx[0] = gy[0] + gy[1] + gy[2] + gy[3]
    xg = [net.push(gx.at[0], gx.at[k], gx.at[k], xdev(k)) for k in (1, 2, 3)]
    over.wait_recv()
    dn16[...] += hin[...]
    rows_out = net.push(
        dn16.at[pl.ds(pl.multiple_of((1 - c) * 8, 8), 8), :], dn.at[c], dn.at[1 - c], sib
    )
    dn[c] = dn16[pl.ds(pl.multiple_of(c * 8, 8), 8), :]
    for arrival in xg:
        arrival.wait_recv()
    sums_out[c] = gx[0] + gx[1] + gx[2] + gx[3]
    last = [net.push(sums_out.at[c], sums_out.at[c], sums_out.at[1 - c], sib)]
    rows_out.wait_recv()
    d_normed = jnp.concatenate([dn[0], dn[1]], axis=1)
    scaled = d_normed * gain[...]
    mean1 = jnp.mean(scaled, axis=-1, keepdims=True)
    mean2 = jnp.mean(scaled * std[...], axis=-1, keepdims=True)
    d_in = inv[:, 0:1] * (scaled - mean1 - std[...] * mean2)
    dx_out[...] = (raw[c, 1] + d_in).astype(bf)
    finish_x(0)
    for u in range(2):
        total = keep[u]
        for k in (1, 2, 3):
            ysums[u, k].wait_recv()
            total += YR[u, k].astype(f32)
        if u == 0:
            total = jnp.transpose(total)
        ut[u] = total
    my_half, its_half = (pl.ds(pl.multiple_of(h * 128, 128), 128) for h in (c, 1 - c))
    my_hid, its_hid = (pl.ds(pl.multiple_of(h * 256, 256), 256) for h in (c, 1 - c))
    last += [
        net.push(ut.at[0, its_half, :], up_out.at[:, my_hid], up_out.at[:, its_hid], sib),
        net.push(ut.at[1, :, its_half], down_out.at[my_hid, :], down_out.at[its_hid, :], sib),
    ]
    mine = [
        pltpu.make_async_copy(ut.at[0, my_half, :], up_out.at[:, my_hid], local.at[0]),
        pltpu.make_async_copy(ut.at[1, :, my_half], down_out.at[my_hid, :], local.at[1]),
    ]
    for copy in mine:
        copy.start()
    for arrival in last:
        arrival.wait_recv()
    for copy in mine:
        copy.wait()
    net.drain()


def shards(tokens, grad_out, norm_gain, norm_bias, up_weight, up_bias, down_weight):
    vmem, hbm = pl.BlockSpec(memory_space=pltpu.VMEM), pl.BlockSpec(memory_space=pltpu.HBM)
    bf, f32 = jnp.bfloat16, jnp.float32
    shape, room = jax.ShapeDtypeStruct, pltpu.VMEM
    input_grad, up_grad, down_grad, sums = pl.pallas_call(
        kernel,
        out_shape=(
            shape((8, 4096), bf), shape((128, 512), f32), shape((512, 128), f32), shape((2, 24, 256), f32),
        ),
        in_specs=[vmem, vmem, hbm, hbm, hbm, hbm, hbm],
        out_specs=(vmem, vmem, vmem, vmem),
        scratch_shapes=[
            room((2, 16, 16, 4096), bf),
            room((16, 16, 4096), bf),
            room((16, 256, 256), bf),
            room((16, 256, 256), bf),
            room((1, 4096), f32),
            room((1, 4096), f32),
            room((1, 512), f32),
            room((2, 2, 8, 4096), f32),
            room((8, 4096), f32),
            room((8, 128), f32),
            room((16, 16, 128), f32),
            room((16, 16, 128), f32),
            room((256, 256), bf),
            room((256, 256), bf),
            room((256, 256), bf),
            room((256, 256), f32),
            room((256, 256), f32),
            room((8, 256, 256), bf),
            room((8, 256, 256), bf),
            room((16, 16, 2048), bf),
            room((8, 2, 16, 2048), bf),
            room((16, 2048), f32),
            room((16, 2048), f32),
            room((16, 2048), f32),
            room((2, 8, 2048), f32),
            room((8, 16, 256), f32),
            room((16, 256), f32),
            room((16, 256), f32),
            room((24, 256), f32),
            room((4, 24, 256), f32),
            room((4, 24, 256), f32),
            room((2, 16, 256, 256), bf),
            room((2, 4, 256, 256), bf),
            room((2, 4, 256, 256), bf),
            room((2, 4, 256, 256), bf),
            room((2, 4, 256, 256), bf),
            room((2, 4, 256, 256), bf),
            room((2, 4, 256, 256), bf),
            room((2, 256, 256), f32),
            room((2, 256, 256), f32),
            pltpu.SemaphoreType.DMA((5,)),
            pltpu.SemaphoreType.DMA((180,)),
            pltpu.SemaphoreType.DMA((180,)),
        ],
        compiler_params=pltpu.CompilerParams(
            collective_id=0, has_side_effects=True, vmem_limit_bytes=63 << 20
        ),
    )(
        tokens, grad_out, norm_gain.reshape(1, 4096), norm_bias.reshape(1, 4096),
        up_weight, up_bias.reshape(1, 512), down_weight,
    )
    return (
        input_grad, up_grad, down_grad, sums[:, 16].reshape(512),
        sums[:, 0:8].reshape(4096), sums[:, 8:16].reshape(4096),
    )


def solution(mesh):
    return jax.shard_map(
        shards,
        mesh=mesh,
        in_specs=(
            P(("tensor", "shard", "replica"), None),
            P(("tensor", "shard", "replica"), None),
            P(),
            P(),
            P("shard", "tensor"),
            P("tensor"),
            P("tensor", "shard"),
        ),
        out_specs=(
            P(("tensor", "shard", "replica"), None),
            P(("shard", "replica"), "tensor"),
            P("tensor", ("shard", "replica")),
            P("tensor"),
            P(),
            P(),
        ),
        check_vma=False,
    )
```

```python
import functools
import jax
import jax.numpy as jnp
from jax import lax
from jax.experimental import pallas as pl
from jax.experimental.pallas import tpu as pltpu
from jax.sharding import PartitionSpec as P

MESH = pl.DeviceIdType.MESH
NX, NY, NZ = 4, 4, 8


OFF = set()


def when(cond, body):
    if cond is None:
        body()
    else:
        pl.when(cond)(body)


class Nul:
    cond = None

    def wait_recv(self):
        pass

    def wait_send(self):
        pass


class Arrival:
    def __init__(self, copy, cond):
        self.copy, self.cond = copy, cond

    def wait_recv(self):
        when(self.cond, self.copy.wait_recv)

    def wait_send(self):
        when(self.cond, self.copy.wait_send)


class Links:
    def __init__(self, send, recv):
        self.send, self.recv, self.count, self.open = send, recv, 0, []

    def push(self, src, dst, landed, device, go=None, come=None):
        root = id(getattr(src, "ref", src))
        if self.groups.get(root, "D") in OFF:
            return Nul()
        slot = self.count
        self.count += 1
        pair = dict(
            send_sem=self.send.at[slot], recv_sem=self.recv.at[slot], device_id=device, device_id_type=MESH
        )
        when(go, pltpu.make_async_remote_copy(src_ref=src, dst_ref=dst, **pair).start)
        arrival = pltpu.make_async_remote_copy(src_ref=src, dst_ref=landed, **pair)
        self.open.append(Arrival(arrival, go))
        return Arrival(arrival, come)

    def drain(self):
        for arrival in self.open:
            arrival.wait_send()
        self.open = []


def place():
    t, s, c = lax.axis_index("tensor"), lax.axis_index("shard"), lax.axis_index("replica")
    return t, s, c, s // NY, s % NY, t // NZ, t % NZ


def greet(devices):
    barrier = pltpu.get_barrier_semaphore()
    for device in devices:
        pl.semaphore_signal(barrier, inc=1, device_id=device, device_id_type=MESH)
    pl.semaphore_wait(barrier, len(devices))


def mm(left, right, dims):
    return lax.dot_general(left, right, (dims, ((), ())), preferred_element_type=jnp.float32)


def kernel(
    tok_in, grad_in, gain_hbm, nbias_hbm, up_in, ubias_hbm, down_in,
    dx_out, up_out, down_out, ub_out, gg_out, bg_out,
    XG, XN, WU, WD, gain, nbias, ubias, raw, std, inv, mu, iv, act_t, dh, dh_t, pre, dact,
    dxp, dxr, dxs, zr, zsum, hin, dn16, dn, gz, gh, gsum, gb, gy, gx,
    P, CH, F, CE, DR, Y, YR, keep, ut, sums, local, send, recv,
):
    bf, f32 = jnp.bfloat16, jnp.float32
    t, s, c, x, yl, yh, z = place()
    sib = {"replica": 1 - c}
    xdev = lambda k: {"shard": ((x + k) % NX) * NY + yl}
    ydev = lambda k: {"shard": x * NY + (yl + k) % NY}
    zdev = lambda k: {"tensor": yh * NZ + (z + k) % NZ}
    opp = {"tensor": (1 - yh) * NZ + z}
    sof = lambda dx, dy: ((x + dx + NX) % NX) * NY + (yl + dy + NY) % NY
    tof = lambda dh, dz: ((yh + dh) % 2) * NZ + (z + dz + NZ) % NZ
    net = Links(send, recv)
    root_of = lambda ref: id(getattr(ref, "ref", ref))
    net.groups = {root_of(r): g for g, rs in {"W": (up_in, down_in, WU, WD), "Z": (XG, raw), "X": (P, F, Y, ut)}.items() for r in rs}

    half = pl.multiple_of(c * 256, 256)
    own_up, own_down = up_in.at[:, pl.ds(half, 256)], down_in.at[pl.ds(half, 256), :]
    mine = [
        pltpu.make_async_copy(own_up, WU.at[s], local.at[0]),
        pltpu.make_async_copy(own_down, WD.at[s], local.at[1]),
        pltpu.make_async_copy(gain_hbm, gain, local.at[2]),
        pltpu.make_async_copy(nbias_hbm, nbias, local.at[3]),
        pltpu.make_async_copy(ubias_hbm, ubias, local.at[4]),
    ]
    for copy in mine:
        copy.start()
    raw[c, 0] = tok_in[...].astype(f32)
    raw[c, 1] = grad_in[...].astype(f32)
    greet([sib, opp] + [xdev(k) for k in (1, 2, 3)] + [ydev(k) for k in (1, 2, 3)] + [zdev(k) for k in range(1, NZ)])
    first = net.push(raw.at[c], raw.at[c], raw.at[1 - c], sib)
    mine[0].wait()
    mine[1].wait()

    has_left, has_right = yl > 0, yl < NY - 1
    line, xin, far = {}, {}, {}

    def there(side, k):
        return yl - 1 - k >= 0 if side < 0 else yl + 1 + k <= NY - 1

    def along(side, k):
        here, landed = sof(0, side * k), sof(0, side * (k + 1))
        if side < 0:
            go = has_right if k == 0 else jnp.logical_and(has_right, yl - k >= 0)
        else:
            go = has_left if k == 0 else jnp.logical_and(has_left, yl + k <= NY - 1)
        line[side, k] = [
            net.push(w.at[here], w.at[here], w.at[landed], ydev(1 if side < 0 else 3), go, there(side, k))
            for w in (WU, WD)
        ]

    def xsend(name, dy, cond):
        here, left, right = sof(0, dy), sof(-1, dy), sof(1, dy)
        xin[name] = [
            net.push(WU.at[here], WU.at[here], WU.at[right], xdev(3), cond, cond),
            net.push(WD.at[here], WD.at[here], WD.at[left], xdev(1), cond, cond),
            net.push(WU.at[here], WU.at[here], WU.at[left], xdev(1), cond, cond),
            net.push(WD.at[here], WD.at[here], WD.at[right], xdev(3), cond, cond),
        ]

    def xforward(name, dy, cond):
        left, right, opposite = sof(-1, dy), sof(1, dy), sof(2, dy)
        xin[name][0].wait_recv()
        one = net.push(WU.at[right], WU.at[right], WU.at[opposite], xdev(3), cond, cond)
        xin[name][1].wait_recv()
        two = net.push(WD.at[left], WD.at[left], WD.at[opposite], xdev(1), cond, cond)
        xin[name][2].wait_recv()
        xin[name][3].wait_recv()
        far[name] = (one, two)

    def yland(k):
        for side in (-1, 1):
            for arrival in line[side, k]:
                arrival.wait_recv()
            if k < 2:
                along(side, k + 1)
            xsend((side, k), side * (k + 1), there(side, k))

    def pass_x(k):
        for side in (-1, 1):
            xforward((side, k), side * (k + 1), there(side, k))

    along(-1, 0)
    along(1, 0)
    xsend("own", 0, None)

    twin, ring = {}, {}

    def part(i, slot, h):
        return XG.at[i, slot, :, pl.ds(h * 2048, 2048)]

    def share(name, slot, h):
        twin.setdefault(name, []).append(net.push(part(c, slot, h), part(c, slot, h), part(1 - c, slot, h), sib))

    def zsend(q, k, h):
        a, b = tof(q, -k), tof(q, k)
        right = net.push(part(c, a, h), part(c, a, h), part(c, tof(q, -k - 1), h), zdev(1)) if k < 3 or q == 0 else None
        left = net.push(part(c, b, h), part(c, b, h), part(c, tof(q, k + 1), h), zdev(7)) if k < 3 or q == 1 else None
        ring[q, k, h] = (right, left)

    def zland(q, k):
        for h in range(2):
            right, left = ring[q, k, h]
            if right is not None:
                right.wait_recv()
            if left is not None:
                left.wait_recv()
            if k < 3:
                zsend(q, k + 1, h)
            if right is not None:
                share(k, tof(q, -k - 1), h)
            if left is not None:
                share(k, tof(q, k + 1), h)

    def normalize(slot):
        wide = XG[0, slot].astype(f32)
        mean = jnp.mean(wide, axis=-1, keepdims=True)
        centred = wide - mean
        istd = lax.rsqrt(jnp.mean(centred * centred, axis=-1, keepdims=True) + 1e-05)
        XN[slot] = (centred * istd * gain[...] + nbias[...]).astype(bf)
        mu[slot] = jnp.broadcast_to(mean, (16, 128))
        iv[slot] = jnp.broadcast_to(istd, (16, 128))

    def settle(k):
        for arrival in twin[k]:
            arrival.wait_recv()
        if k == "y":
            normalize(tof(1, 0))
        elif k < 3:

            @pl.loop(0, 4)
            def _(i):
                normalize(((yh + i // 2) % 2) * NZ + (z + (2 * (i % 2) - 1) * (k + 1) + NZ) % NZ)
        else:

            @pl.loop(0, 2)
            def _(i):
                normalize(((yh + i) % 2) * NZ + (z + 4) % NZ)

    first.wait_recv()
    for i in range(2):
        XG[i, t] = jnp.concatenate([raw[0, i], raw[1, i]], axis=0).astype(bf)
    over = [net.push(part(c, t, h), part(c, t, h), part(c, tof(1, 0), h), opp) for h in range(2)]
    for h in range(2):
        zsend(0, 0, h)
    for copy in mine[2:]:
        copy.wait()
    normalize(t)
    yland(0)
    for h in range(2):
        over[h].wait_recv()
        zsend(1, 0, h)
        share("y", tof(1, 0), h)
    zland(0, 0)
    xforward("own", 0, None)
    zland(1, 0)
    yland(1)
    settle("y")
    zland(0, 1)
    pass_x(0)
    zland(1, 1)
    yland(2)
    settle(0)
    zland(0, 2)
    zland(1, 2)
    settle(1)
    pass_x(1)
    zland(0, 3)
    zland(1, 3)
    settle(2)
    wide = raw[c, 0]
    centred = wide - jnp.mean(wide, axis=-1, keepdims=True)
    istd = lax.rsqrt(jnp.mean(centred * centred, axis=-1, keepdims=True) + 1e-05)
    inv[...] = jnp.broadcast_to(istd, inv.shape)
    std[...] = centred * istd
    settle(3)

    def forward(s1):
        cols = pl.ds(pl.multiple_of(s1 * 256, 256), 256)
        pre[...] += mm(XN[:, :, cols].reshape(256, 256), WU[s1], ((1,), (0,)))
        dact[...] += mm(XG[1, :, :, cols].reshape(256, 256), WD[s1], ((1,), (1,)))

    pre[...] = jnp.broadcast_to(ubias[:, pl.ds(half, 256)], pre.shape)
    dact[...] = jnp.zeros_like(dact)
    remote = lambda y1: jnp.abs(y1 - yl) == 3
    near = lambda i, y1: ((x + i + i // 2) % NX) * NY + y1

    @pl.loop(0, 12)
    def _(i):
        @pl.when(jnp.logical_not(remote(i // 3)))
        def _():
            forward(near(i % 3, i // 3))

    pass_x(2)
    for name in ("own", (-1, 0), (1, 0), (-1, 1), (1, 1)):
        for arrival in far[name]:
            arrival.wait_recv()

    @pl.loop(0, 4)
    def _(y1):
        @pl.when(jnp.logical_not(remote(y1)))
        def _():
            forward(((x + 2) % NX) * NY + y1)

    ends_line = jnp.logical_or(yl == 0, yl == 3)

    @pl.when(ends_line)
    def _():
        @pl.loop(0, 3)
        def _(i):
            forward(near(i, 3 - yl))

    for name in ((-1, 2), (1, 2)):
        for arrival in far[name]:
            arrival.wait_recv()

    @pl.when(ends_line)
    def _():
        forward(((x + 2) % NX) * NY + 3 - yl)

    v = pre[...]
    root = 0.7978845608028654
    th = jnp.tanh(root * (v + 0.044715 * v * v * v))
    slope = 0.5 * (1.0 + th) + 0.5 * v * (1.0 - th * th) * (root * (1.0 + 3 * 0.044715 * v * v))
    grad_pre = (dact[...] * slope).astype(bf)
    dh[...] = grad_pre

    wide_pre = grad_pre.astype(f32)
    dh_t[...] = jnp.transpose(wide_pre).astype(bf)
    act_t[...] = jnp.transpose(0.5 * v * (1.0 + th)).astype(bf)
    gb[16:24, :] = jnp.broadcast_to(jnp.sum(wide_pre, axis=0, keepdims=True), (8, 256))

    chain, direct, ends, ysums = {}, {}, {}, {}

    def partials(k):
        @pl.loop(0, 4)
        def _(i):
            s1 = i * NY + (yl + k) % NY
            cols = pl.ds(pl.multiple_of(s1 * 256, 256), 256)
            P[0, s1] = mm(dh_t[...], XN[:, :, cols].reshape(256, 256), ((1,), (0,))).astype(bf)
            P[1, s1] = mm(act_t[...], XG[1, :, :, cols].reshape(256, 256), ((1,), (0,))).astype(bf)

        chain[k] = (
            net.push(P.at[0, sof(2, k)], CH.at[0, k], CH.at[0, k], xdev(3)),
            net.push(P.at[1, sof(2, k)], CH.at[1, k], CH.at[1, k], xdev(1)),
        )
        direct[k] = (
            net.push(P.at[0, sof(1, k)], DR.at[0, k], DR.at[0, k], xdev(1)),
            net.push(P.at[1, sof(-1, k)], DR.at[1, k], DR.at[1, k], xdev(3)),
        )

    def pass_on(k):
        for u, (dx, device) in enumerate(((-1, xdev(3)), (1, xdev(1)))):
            chain[k][u].wait_recv()
            F[u, k] = (CH[u, k].astype(f32) + P[u, sof(dx, k)].astype(f32)).astype(bf)
            ends[u, k] = net.push(F.at[u, k], CE.at[u, k], CE.at[u, k], device)

    def finish_x(k):
        for u in range(2):
            direct[k][u].wait_recv()
            ends[u, k].wait_recv()
            total = P[u, sof(0, k)].astype(f32) + CE[u, k].astype(f32) + DR[u, k].astype(f32)
            if k == 0:
                keep[u] = total
            else:
                Y[u, k] = total.astype(bf)
                ysums[u, k] = net.push(Y.at[u, k], YR.at[u, k], YR.at[u, k], ydev(k))

    partials(2)
    @pl.loop(0, 8)
    def _(i):
        dxp[i] = mm(dh[...], WU[(1 - c) * 8 + i], ((1,), (1,))).astype(bf)

    dx_in = net.push(dxp, dxr, dxr, sib)
    partials(1)
    dx_in.wait_recv()

    @pl.loop(0, 8)
    def _(i):
        total = mm(dh[...], WU[c * 8 + i], ((1,), (1,))) + dxr[i].astype(f32)
        dxs[:, :, pl.ds(pl.multiple_of(i * 256, 256), 256)] = total.astype(bf).reshape(16, 16, 256)
        cols = pl.ds(pl.multiple_of((c * 8 + i) * 256, 256), 256)
        tok = XG[0, :, :, cols].reshape(256, 256).astype(f32)
        standard = (tok - mu[...].reshape(256, 128)[:, 0:1]) * iv[...].reshape(256, 128)[:, 0:1]
        gsum[pl.ds(i, 1), :] = jnp.sum(total * standard, axis=0, keepdims=True)
        gsum[pl.ds(8 + i, 1), :] = jnp.sum(total, axis=0, keepdims=True)

    zg = [net.push(gsum, gz.at[k], gz.at[k], zdev(k)) for k in range(1, NZ)]
    zin = []
    for k in (4, 3, 5, 2, 6, 1, 7):
        for h in range(2):
            zin.append(net.push(dxs.at[h * NZ + (z + k) % NZ], zr.at[k, h], zr.at[k, h], zdev(k)))
    pass_on(2)
    partials(3)
    pass_on(1)
    finish_x(2)
    partials(0)
    total = gsum[...]
    for k, arrival in enumerate(zg, 1):
        arrival.wait_recv()
        total += gz[k]
    gb[0:16, :] = total
    hg = net.push(gb.at[0:16, :], gh, gh, opp)
    pass_on(3)
    finish_x(1)
    hg.wait_recv()
    gy[0, 16:24, :] = gb[16:24, :]
    gy[0, 0:16, :] = gb[0:16, :] + gh[...]
    yg = [net.push(gy.at[0], gy.at[k], gy.at[k], ydev(k)) for k in (1, 2, 3)]

    for arrival in zin:
        arrival.wait_recv()

    def zadd(h):
        total = dxs[h * NZ + z].astype(f32)
        for k in range(1, NZ):
            total += zr[k, h].astype(f32)
        return total

    zsum[...] = zadd(1 - yh)
    over = net.push(zsum, hin, hin, opp)
    dn16[...] = zadd(yh)
    pass_on(0)
    finish_x(3)
    for arrival in yg:
        arrival.wait_recv()
    gx[0] = gy[0] + gy[1] + gy[2] + gy[3]
    xg = [net.push(gx.at[0], gx.at[k], gx.at[k], xdev(k)) for k in (1, 2, 3)]
    over.wait_recv()
    dn16[...] += hin[...]
    rows_out = net.push(
        dn16.at[pl.ds(pl.multiple_of((1 - c) * 8, 8), 8), :], dn.at[c], dn.at[1 - c], sib
    )
    dn[c] = dn16[pl.ds(pl.multiple_of(c * 8, 8), 8), :]
    for arrival in xg:
        arrival.wait_recv()
    sums[c] = gx[0] + gx[1] + gx[2] + gx[3]
    last = [net.push(sums.at[c], sums.at[c], sums.at[1 - c], sib)]
    rows_out.wait_recv()
    d_normed = jnp.concatenate([dn[0], dn[1]], axis=1)
    scaled = d_normed * gain[...]
    mean1 = jnp.mean(scaled, axis=-1, keepdims=True)
    mean2 = jnp.mean(scaled * std[...], axis=-1, keepdims=True)
    d_in = inv[:, 0:1] * (scaled - mean1 - std[...] * mean2)
    dx_out[...] = (raw[c, 1] + d_in).astype(bf)
    finish_x(0)
    for u in range(2):
        total = keep[u]
        for k in (1, 2, 3):
            ysums[u, k].wait_recv()
            total += YR[u, k].astype(f32)
        if u == 0:
            total = jnp.transpose(total)
        ut[u] = total
    my_half, its_half = (pl.ds(pl.multiple_of(h * 128, 128), 128) for h in (c, 1 - c))
    my_hid, its_hid = (pl.ds(pl.multiple_of(h * 256, 256), 256) for h in (c, 1 - c))
    last += [
        net.push(ut.at[0, its_half, :], up_out.at[:, my_hid], up_out.at[:, its_hid], sib),
        net.push(ut.at[1, :, its_half], down_out.at[my_hid, :], down_out.at[its_hid, :], sib),
    ]
    mine = [
        pltpu.make_async_copy(ut.at[0, my_half, :], up_out.at[:, my_hid], local.at[0]),
        pltpu.make_async_copy(ut.at[1, :, my_half], down_out.at[my_hid, :], local.at[1]),
    ]
    for copy in mine:
        copy.start()
    last[0].wait_recv()
    for h in range(2):
        ub_out[:, h * 256 : (h + 1) * 256] = sums[h, 16:17, :]
        for i in range(8):
            cols = slice(h * 2048 + i * 256, h * 2048 + (i + 1) * 256)
            gg_out[:, cols] = sums[h, i : i + 1, :]
            bg_out[:, cols] = sums[h, 8 + i : 9 + i, :]
    for arrival in last[1:]:
        arrival.wait_recv()
    for copy in mine:
        copy.wait()
    net.drain()


def hand_over(*refs):
    for source, result in zip(refs[:6], refs[6:]):
        result[...] = source[...]


def shards(tokens, grad_out, norm_gain, norm_bias, up_weight, up_bias, down_weight):
    vmem, hbm = pl.BlockSpec(memory_space=pltpu.VMEM), pl.BlockSpec(memory_space=pltpu.HBM)
    bf, f32 = jnp.bfloat16, jnp.float32
    shape, room = jax.ShapeDtypeStruct, pltpu.VMEM
    outs = pl.pallas_call(
        kernel,
        out_shape=(
            shape((8, 4096), bf), shape((128, 512), f32), shape((512, 128), f32),
            shape((1, 512), f32), shape((1, 4096), f32), shape((1, 4096), f32),
        ),
        in_specs=[vmem, vmem, hbm, hbm, hbm, hbm, hbm],
        out_specs=(vmem,) * 6,
        scratch_shapes=[
            room((2, 16, 16, 4096), bf),
            room((16, 16, 4096), bf),
            room((16, 256, 256), bf),
            room((16, 256, 256), bf),
            room((1, 4096), f32),
            room((1, 4096), f32),
            room((1, 512), f32),
            room((2, 2, 8, 4096), f32),
            room((8, 4096), f32),
            room((8, 128), f32),
            room((16, 16, 128), f32),
            room((16, 16, 128), f32),
            room((256, 256), bf),
            room((256, 256), bf),
            room((256, 256), bf),
            room((256, 256), f32),
            room((256, 256), f32),
            room((8, 256, 256), bf),
            room((8, 256, 256), bf),
            room((16, 16, 2048), bf),
            room((8, 2, 16, 2048), bf),
            room((16, 2048), f32),
            room((16, 2048), f32),
            room((16, 2048), f32),
            room((2, 8, 2048), f32),
            room((8, 16, 256), f32),
            room((16, 256), f32),
            room((16, 256), f32),
            room((24, 256), f32),
            room((4, 24, 256), f32),
            room((4, 24, 256), f32),
            room((2, 16, 256, 256), bf),
            room((2, 4, 256, 256), bf),
            room((2, 4, 256, 256), bf),
            room((2, 4, 256, 256), bf),
            room((2, 4, 256, 256), bf),
            room((2, 4, 256, 256), bf),
            room((2, 4, 256, 256), bf),
            room((2, 256, 256), f32),
            room((2, 256, 256), f32),
            room((2, 24, 256), f32),
            pltpu.SemaphoreType.DMA((5,)),
            pltpu.SemaphoreType.DMA((220,)),
            pltpu.SemaphoreType.DMA((220,)),
        ],
        compiler_params=pltpu.CompilerParams(
            collective_id=0, has_side_effects=True, vmem_limit_bytes=63 << 20
        ),
    )(
        tokens, grad_out, norm_gain.reshape(1, 4096), norm_bias.reshape(1, 4096),
        up_weight, up_bias.reshape(1, 512), down_weight,
    )
    outs = pl.pallas_call(
        hand_over,
        out_shape=tuple(shape(out.shape, out.dtype) for out in outs),
        in_specs=[vmem] * 6,
        out_specs=(vmem,) * 6,
    )(*outs)
    input_grad, up_grad, down_grad, up_bias_grad, gain_grad, bias_grad = outs
    return (
        input_grad, up_grad, down_grad, up_bias_grad.reshape(512), gain_grad.reshape(4096), bias_grad.reshape(4096),
    )


def solution(mesh):
    return jax.shard_map(
        shards,
        mesh=mesh,
        in_specs=(
            P(("tensor", "shard", "replica"), None),
            P(("tensor", "shard", "replica"), None),
            P(),
            P(),
            P("shard", "tensor"),
            P("tensor"),
            P("tensor", "shard"),
        ),
        out_specs=(
            P(("tensor", "shard", "replica"), None),
            P(("shard", "replica"), "tensor"),
            P("tensor", ("shard", "replica")),
            P("tensor"),
            P(),
            P(),
        ),
        check_vma=False,
    )
```

```python
import functools
import jax
import jax.numpy as jnp
from jax import lax
from jax.experimental import pallas as pl
from jax.experimental.pallas import tpu as pltpu
from jax.sharding import PartitionSpec as P

MESH = pl.DeviceIdType.MESH
NX, NY, NZ = 4, 4, 8


def when(cond, body):
    if cond is None:
        body()
    else:
        pl.when(cond)(body)


class Arrival:
    def __init__(self, copy, cond):
        self.copy, self.cond = copy, cond

    def wait_recv(self):
        when(self.cond, self.copy.wait_recv)

    def wait_send(self):
        when(self.cond, self.copy.wait_send)


class Links:
    def __init__(self, send, recv):
        self.send, self.recv, self.count, self.open = send, recv, 0, []

    def push(self, src, dst, landed, device, go=None, come=None):
        slot = self.count
        self.count += 1
        pair = dict(
            send_sem=self.send.at[slot], recv_sem=self.recv.at[slot], device_id=device, device_id_type=MESH
        )
        when(go, pltpu.make_async_remote_copy(src_ref=src, dst_ref=dst, **pair).start)
        arrival = pltpu.make_async_remote_copy(src_ref=src, dst_ref=landed, **pair)
        self.open.append(Arrival(arrival, go))
        return Arrival(arrival, come)

    def drain(self):
        for arrival in self.open:
            arrival.wait_send()
        self.open = []


def place():
    t, s, c = lax.axis_index("tensor"), lax.axis_index("shard"), lax.axis_index("replica")
    return t, s, c, s // NY, s % NY, t // NZ, t % NZ


def greet(devices):
    barrier = pltpu.get_barrier_semaphore()
    for device in devices:
        pl.semaphore_signal(barrier, inc=1, device_id=device, device_id_type=MESH)
    pl.semaphore_wait(barrier, len(devices))


def mm(left, right, dims):
    return lax.dot_general(left, right, (dims, ((), ())), preferred_element_type=jnp.float32)


def kernel(
    tok_in, grad_in, gain_hbm, nbias_hbm, up_in, ubias_hbm, down_in,
    dx_out, up_out, down_out, ub_out, gg_out, bg_out,
    A, XN, W, gain, nbias, ubias, raw, std, inv, mu, iv, act_t, lt, dh, acc, dacc,
    dxs, zr, zsum, hin, dn16, dn, gz, gh, gsum, gb, gy, gx,
    P, CH, F, CE, DR, Y, YR, keep, ut, sums, local, send, recv,
):
    bf, f32 = jnp.bfloat16, jnp.float32
    t, s, c, x, yl, yh, z = place()
    sib = {"replica": 1 - c}
    xdev = lambda k: {"shard": ((x + k) % NX) * NY + yl}
    ydev = lambda k: {"shard": x * NY + (yl + k) % NY}
    zdev = lambda k: {"tensor": yh * NZ + (z + k) % NZ}
    opp = {"tensor": (1 - yh) * NZ + z}
    sof = lambda dx, dy: ((x + dx + NX) % NX) * NY + (yl + dy + NY) % NY
    tof = lambda dh, dz: ((yh + dh) % 2) * NZ + (z + dz + NZ) % NZ
    net = Links(send, recv)
    first_core, second_core = c == 0, c == 1

    def own_weights(act):
        for core, take in (
            (first_core, lambda h: up_in.at[:, pl.ds(h * 256, 256)]),
            (second_core, lambda h: down_in.at[pl.ds(h * 256, 256), :]),
        ):

            @pl.when(core)
            def _():
                for h in range(2):
                    act(pltpu.make_async_copy(take(h), W.at[s, h], local.at[h]))

    mine = [
        pltpu.make_async_copy(gain_hbm, gain, local.at[2]),
        pltpu.make_async_copy(nbias_hbm, nbias, local.at[3]),
        pltpu.make_async_copy(ubias_hbm, ubias, local.at[4]),
    ]
    own_weights(lambda copy: copy.start())
    for copy in mine:
        copy.start()
    raw[c, 0] = tok_in[...].astype(f32)
    raw[c, 1] = grad_in[...].astype(f32)
    greet([sib, opp] + [xdev(k) for k in (1, 2, 3)] + [ydev(k) for k in (1, 2, 3)] + [zdev(k) for k in range(1, NZ)])
    first = net.push(raw.at[c, 1 - c], raw.at[c, 1 - c], raw.at[1 - c, c], sib)
    own_weights(lambda copy: copy.wait())

    has_left, has_right = yl > 0, yl < NY - 1
    line, xin, far = {}, {}, {}

    def there(side, k):
        return yl - 1 - k >= 0 if side < 0 else yl + 1 + k <= NY - 1

    def along(side, k):
        here, landed = sof(0, side * k), sof(0, side * (k + 1))
        if side < 0:
            go = has_right if k == 0 else jnp.logical_and(has_right, yl - k >= 0)
        else:
            go = has_left if k == 0 else jnp.logical_and(has_left, yl + k <= NY - 1)
        line[side, k] = net.push(W.at[here], W.at[here], W.at[landed], ydev(1 if side < 0 else 3), go, there(side, k))

    def xsend(name, dy, cond):
        here, left, right = sof(0, dy), sof(-1, dy), sof(1, dy)
        xin[name] = [
            net.push(W.at[here, 0], W.at[here, 0], W.at[right, 0], xdev(3), cond, cond),
            net.push(W.at[here, 1], W.at[here, 1], W.at[left, 1], xdev(1), cond, cond),
            net.push(W.at[here, 0], W.at[here, 0], W.at[left, 0], xdev(1), cond, cond),
            net.push(W.at[here, 1], W.at[here, 1], W.at[right, 1], xdev(3), cond, cond),
        ]

    def xforward(name, dy, cond):
        left, right, opposite = sof(-1, dy), sof(1, dy), sof(2, dy)
        xin[name][0].wait_recv()
        one = net.push(W.at[right, 0], W.at[right, 0], W.at[opposite, 0], xdev(3), cond, cond)
        xin[name][1].wait_recv()
        two = net.push(W.at[left, 1], W.at[left, 1], W.at[opposite, 1], xdev(1), cond, cond)
        xin[name][2].wait_recv()
        xin[name][3].wait_recv()
        far[name] = (one, two)

    def yland(k):
        for side in (-1, 1):
            line[side, k].wait_recv()
            if k < 2:
                along(side, k + 1)
            xsend((side, k), side * (k + 1), there(side, k))

    def pass_x(k):
        for side in (-1, 1):
            xforward((side, k), side * (k + 1), there(side, k))

    along(-1, 0)
    along(1, 0)
    xsend("own", 0, None)

    ring = {}

    def part(slot, h):
        return A.at[slot, :, pl.ds(h * 2048, 2048)]

    def zsend(q, k, h):
        a, b = tof(q, -k), tof(q, k)
        right = net.push(part(a, h), part(a, h), part(tof(q, -k - 1), h), zdev(1)) if k < 3 or q == 0 else None
        left = net.push(part(b, h), part(b, h), part(tof(q, k + 1), h), zdev(7)) if k < 3 or q == 1 else None
        ring[q, k, h] = (right, left)

    def zland(q, k):
        for h in range(2):
            for arrival in ring[q, k, h]:
                if arrival is not None:
                    arrival.wait_recv()
            if k < 3:
                zsend(q, k + 1, h)

    def normalize(slot):
        @pl.when(first_core)
        def _():
            wide = A[slot].astype(f32)
            mean = jnp.mean(wide, axis=-1, keepdims=True)
            centred = wide - mean
            istd = lax.rsqrt(jnp.mean(centred * centred, axis=-1, keepdims=True) + 1e-05)
            XN[slot] = (centred * istd * gain[...] + nbias[...]).astype(bf)
            mu[slot] = jnp.broadcast_to(mean, (16, 128))
            iv[slot] = jnp.broadcast_to(istd, (16, 128))

        @pl.when(second_core)
        def _():
            XN[slot] = A[slot]

    def settle(k):
        if k == "y":
            normalize(tof(1, 0))
        elif k < 3:

            @pl.loop(0, 4)
            def _(i):
                normalize(((yh + i // 2) % 2) * NZ + (z + (2 * (i % 2) - 1) * (k + 1) + NZ) % NZ)
        else:

            @pl.loop(0, 2)
            def _(i):
                normalize(((yh + i) % 2) * NZ + (z + 4) % NZ)

    first.wait_recv()
    A[t] = jnp.concatenate([raw[0, c], raw[1, c]], axis=0).astype(bf)
    over = [net.push(part(t, h), part(t, h), part(tof(1, 0), h), opp) for h in range(2)]
    for h in range(2):
        zsend(0, 0, h)
    for copy in mine:
        copy.wait()
    normalize(t)
    yland(0)
    for h in range(2):
        over[h].wait_recv()
        zsend(1, 0, h)
    zland(0, 0)
    xforward("own", 0, None)
    zland(1, 0)
    yland(1)
    settle("y")
    zland(0, 1)
    pass_x(0)
    zland(1, 1)
    yland(2)
    settle(0)
    zland(0, 2)
    zland(1, 2)
    settle(1)
    pass_x(1)
    zland(0, 3)
    zland(1, 3)
    settle(2)
    wide = raw[c, 0]
    centred = wide - jnp.mean(wide, axis=-1, keepdims=True)
    istd = lax.rsqrt(jnp.mean(centred * centred, axis=-1, keepdims=True) + 1e-05)
    inv[...] = jnp.broadcast_to(istd, inv.shape)
    std[...] = centred * istd
    settle(3)

    def forward(s1):
        cols = pl.ds(pl.multiple_of(s1 * 256, 256), 256)
        for core, dims in ((first_core, ((1,), (0,))), (second_core, ((1,), (1,)))):

            @pl.when(core)
            def _():
                right = XN[:, :, cols].reshape(256, 256)
                for h in range(2):
                    acc[h] += mm(right, W[s1, h], dims)

    for h in range(2):
        start = jnp.where(first_core, ubias[:, h * 256 : (h + 1) * 256], 0.0)
        acc[h] = jnp.broadcast_to(start, (256, 256))
    remote = lambda y1: jnp.abs(y1 - yl) == 3
    near = lambda i, y1: ((x + i + i // 2) % NX) * NY + y1

    @pl.loop(0, 12)
    def _(i):
        @pl.when(jnp.logical_not(remote(i // 3)))
        def _():
            forward(near(i % 3, i // 3))

    pass_x(2)
    for name in ("own", (-1, 0), (1, 0), (-1, 1), (1, 1)):
        for arrival in far[name]:
            arrival.wait_recv()

    @pl.loop(0, 4)
    def _(y1):
        @pl.when(jnp.logical_not(remote(y1)))
        def _():
            forward(((x + 2) % NX) * NY + y1)

    ends_line = jnp.logical_or(yl == 0, yl == 3)

    @pl.when(ends_line)
    def _():
        @pl.loop(0, 3)
        def _(i):
            forward(near(i, 3 - yl))

    for name in ((-1, 2), (1, 2)):
        for arrival in far[name]:
            arrival.wait_recv()

    @pl.when(ends_line)
    def _():
        forward(((x + 2) % NX) * NY + 3 - yl)

    d_act_in = net.push(acc, dacc, dacc, sib, second_core, first_core)

    @pl.when(first_core)
    def _():
        root = 0.7978845608028654
        for h in range(2):
            v = acc[h]
            th = jnp.tanh(root * (v + 0.044715 * v * v * v))
            act_t[h] = jnp.transpose(0.5 * v * (1.0 + th)).astype(bf)
            acc[h] = 0.5 * (1.0 + th) + 0.5 * v * (1.0 - th * th) * (root * (1.0 + 3 * 0.044715 * v * v))

    act_in = net.push(act_t, lt, lt, sib, first_core, second_core)
    d_act_in.wait_recv()

    @pl.when(first_core)
    def _():
        gb[32:40, :] = jnp.zeros((8, 256), f32)
        for h in range(2):
            d_pre = (dacc[h] * acc[h]).astype(bf)
            dh[h] = d_pre
            lt[h] = jnp.transpose(d_pre.astype(f32)).astype(bf)
            gb[32 + h : 33 + h, :] = jnp.sum(d_pre.astype(f32), axis=0, keepdims=True)

    act_in.wait_recv()

    chain, direct, ends, ysums = {}, {}, {}, {}

    def partials(k):
        @pl.loop(0, 4)
        def _(i):
            s1 = i * NY + (yl + k) % NY
            cols = pl.ds(pl.multiple_of(s1 * 256, 256), 256)
            right = XN[:, :, cols].reshape(256, 256)
            for h in range(2):
                P[h, s1] = mm(lt[h], right, ((1,), (0,))).astype(bf)

        chain[k] = (
            net.push(P.at[0, sof(2, k)], CH.at[0, k], CH.at[0, k], xdev(3)),
            net.push(P.at[1, sof(2, k)], CH.at[1, k], CH.at[1, k], xdev(1)),
        )
        direct[k] = (
            net.push(P.at[0, sof(1, k)], DR.at[0, k], DR.at[0, k], xdev(1)),
            net.push(P.at[1, sof(-1, k)], DR.at[1, k], DR.at[1, k], xdev(3)),
        )

    def pass_on(k):
        for u, (dx, device) in enumerate(((-1, xdev(3)), (1, xdev(1)))):
            chain[k][u].wait_recv()
            F[u, k] = (CH[u, k].astype(f32) + P[u, sof(dx, k)].astype(f32)).astype(bf)
            ends[u, k] = net.push(F.at[u, k], CE.at[u, k], CE.at[u, k], device)

    def finish_x(k):
        for u in range(2):
            direct[k][u].wait_recv()
            ends[u, k].wait_recv()
            total = P[u, sof(0, k)].astype(f32) + CE[u, k].astype(f32) + DR[u, k].astype(f32)
            if k == 0:
                keep[u] = total
            else:
                Y[u, k] = total.astype(bf)
                ysums[u, k] = net.push(Y.at[u, k], YR.at[u, k], YR.at[u, k], ydev(k))

    def d_normed_part(j):
        @pl.when(first_core)
        def _():
            @pl.loop(0, 8)
            def _(i):
                block = j * 8 + i
                total = mm(dh[0], W[block, 0], ((1,), (1,))) + mm(dh[1], W[block, 1], ((1,), (1,)))
                dxs[j, :, :, pl.ds(pl.multiple_of(i * 256, 256), 256)] = total.astype(bf).reshape(16, 16, 256)
                tok = A[:, :, pl.ds(pl.multiple_of(block * 256, 256), 256)].reshape(256, 256).astype(f32)
                standard = (tok - mu[...].reshape(256, 128)[:, 0:1]) * iv[...].reshape(256, 128)[:, 0:1]
                gsum[pl.ds(block, 1), :] = jnp.sum(total * standard, axis=0, keepdims=True)
                gsum[pl.ds(16 + block, 1), :] = jnp.sum(total, axis=0, keepdims=True)

        for k in (4, 3, 5, 2, 6, 1, 7):
            for h in range(2):
                zin.append(
                    net.push(
                        dxs.at[j, h * NZ + (z + k) % NZ], zr.at[k, h, j], zr.at[k, h, j], zdev(k), first_core, first_core
                    )
                )

    zin = []
    partials(2)
    d_normed_part(0)
    partials(1)
    d_normed_part(1)
    zg = [net.push(gsum, gz.at[k], gz.at[k], zdev(k), first_core, first_core) for k in range(1, NZ)]
    pass_on(2)
    partials(3)
    pass_on(1)
    finish_x(2)
    partials(0)
    for arrival in zg:
        arrival.wait_recv()

    @pl.when(first_core)
    def _():
        total = gsum[...]
        for k in range(1, NZ):
            total += gz[k]
        gb[0:32, :] = total

    hg = net.push(gb.at[0:32, :], gh, gh, opp, first_core, first_core)
    pass_on(3)
    finish_x(1)
    hg.wait_recv()

    @pl.when(first_core)
    def _():
        gy[0, 32:40, :] = gb[32:40, :]
        gy[0, 0:32, :] = gb[0:32, :] + gh[...]

    yg = [net.push(gy.at[0], gy.at[k], gy.at[k], ydev(k), first_core, first_core) for k in (1, 2, 3)]

    for arrival in zin:
        arrival.wait_recv()

    def zadd(h, j):
        total = dxs[j, h * NZ + z].astype(f32)
        for k in range(1, NZ):
            total += zr[k, h, j].astype(f32)
        return total

    @pl.when(first_core)
    def _():
        for j in range(2):
            zsum[j] = zadd(1 - yh, j)

    over = net.push(zsum, hin, hin, opp, first_core, first_core)

    @pl.when(first_core)
    def _():
        for j in range(2):
            dn16[j] = zadd(yh, j)

    pass_on(0)
    finish_x(3)
    for arrival in yg:
        arrival.wait_recv()

    @pl.when(first_core)
    def _():
        gx[0] = gy[0] + gy[1] + gy[2] + gy[3]

    xg = [net.push(gx.at[0], gx.at[k], gx.at[k], xdev(k), first_core, first_core) for k in (1, 2, 3)]
    over.wait_recv()

    @pl.when(first_core)
    def _():
        for j in range(2):
            dn16[j] += hin[j]
            dn[j] = dn16[j, 0:8, :]

    rows_out = net.push(dn16.at[:, 8:16, :], dn, dn, sib, first_core, second_core)
    for arrival in xg:
        arrival.wait_recv()

    @pl.when(first_core)
    def _():
        sums[...] = gx[0] + gx[1] + gx[2] + gx[3]

    last = [net.push(sums, sums, sums, sib, first_core, second_core)]
    rows_out.wait_recv()
    d_normed = jnp.concatenate([dn[0], dn[1]], axis=1)
    scaled = d_normed * gain[...]
    mean1 = jnp.mean(scaled, axis=-1, keepdims=True)
    mean2 = jnp.mean(scaled * std[...], axis=-1, keepdims=True)
    d_in = inv[:, 0:1] * (scaled - mean1 - std[...] * mean2)
    dx_out[...] = (raw[c, 1] + d_in).astype(bf)
    finish_x(0)
    for u in range(2):
        total = keep[u]
        for k in (1, 2, 3):
            ysums[u, k].wait_recv()
            total += YR[u, k].astype(f32)

        @pl.when(first_core)
        def _():
            ut[u] = jnp.transpose(total)

        @pl.when(second_core)
        def _():
            ut[u] = total

    def own_grads(act):
        @pl.when(first_core)
        def _():
            for h in range(2):
                act(pltpu.make_async_copy(ut.at[h, 0:128, :], up_out.at[:, pl.ds(h * 256, 256)], local.at[h]))

        @pl.when(second_core)
        def _():
            for h in range(2):
                act(pltpu.make_async_copy(ut.at[h, :, 128:256], down_out.at[pl.ds(h * 256, 256), :], local.at[h]))

    for h in range(2):
        up_part, down_part = up_out.at[:, pl.ds(h * 256, 256)], down_out.at[pl.ds(h * 256, 256), :]
        last.append(net.push(ut.at[h, 128:256, :], up_part, up_part, sib, first_core, second_core))
        last.append(net.push(ut.at[h, :, 0:128], down_part, down_part, sib, second_core, first_core))
    own_grads(lambda copy: copy.start())
    last[0].wait_recv()
    for h in range(2):
        ub_out[:, h * 256 : (h + 1) * 256] = sums[32 + h : 33 + h, :]
    for i in range(16):
        cols = slice(i * 256, (i + 1) * 256)
        gg_out[:, cols] = sums[i : i + 1, :]
        bg_out[:, cols] = sums[16 + i : 17 + i, :]
    for arrival in last[1:]:
        arrival.wait_recv()
    own_grads(lambda copy: copy.wait())
    net.drain()


def hand_over(*refs):
    for source, result in zip(refs[:6], refs[6:]):
        result[...] = source[...]


def shards(tokens, grad_out, norm_gain, norm_bias, up_weight, up_bias, down_weight):
    vmem, hbm = pl.BlockSpec(memory_space=pltpu.VMEM), pl.BlockSpec(memory_space=pltpu.HBM)
    bf, f32 = jnp.bfloat16, jnp.float32
    shape, room = jax.ShapeDtypeStruct, pltpu.VMEM
    outs = pl.pallas_call(
        kernel,
        out_shape=(
            shape((8, 4096), bf), shape((128, 512), f32), shape((512, 128), f32),
            shape((1, 512), f32), shape((1, 4096), f32), shape((1, 4096), f32),
        ),
        in_specs=[vmem, vmem, hbm, hbm, hbm, hbm, hbm],
        out_specs=(vmem,) * 6,
        scratch_shapes=[
            room((16, 16, 4096), bf),
            room((16, 16, 4096), bf),
            room((16, 2, 256, 256), bf),
            room((1, 4096), f32),
            room((1, 4096), f32),
            room((1, 512), f32),
            room((2, 2, 8, 4096), f32),
            room((8, 4096), f32),
            room((8, 128), f32),
            room((16, 16, 128), f32),
            room((16, 16, 128), f32),
            room((2, 256, 256), bf),
            room((2, 256, 256), bf),
            room((2, 256, 256), bf),
            room((2, 256, 256), f32),
            room((2, 256, 256), f32),
            room((2, 16, 16, 2048), bf),
            room((8, 2, 2, 16, 2048), bf),
            room((2, 16, 2048), f32),
            room((2, 16, 2048), f32),
            room((2, 16, 2048), f32),
            room((2, 8, 2048), f32),
            room((8, 32, 256), f32),
            room((32, 256), f32),
            room((32, 256), f32),
            room((40, 256), f32),
            room((4, 40, 256), f32),
            room((4, 40, 256), f32),
            room((2, 16, 256, 256), bf),
            room((2, 4, 256, 256), bf),
            room((2, 4, 256, 256), bf),
            room((2, 4, 256, 256), bf),
            room((2, 4, 256, 256), bf),
            room((2, 4, 256, 256), bf),
            room((2, 4, 256, 256), bf),
            room((2, 256, 256), f32),
            room((2, 256, 256), f32),
            room((40, 256), f32),
            pltpu.SemaphoreType.DMA((5,)),
            pltpu.SemaphoreType.DMA((220,)),
            pltpu.SemaphoreType.DMA((220,)),
        ],
        compiler_params=pltpu.CompilerParams(
            collective_id=0, has_side_effects=True, vmem_limit_bytes=63 << 20
        ),
    )(
        tokens, grad_out, norm_gain.reshape(1, 4096), norm_bias.reshape(1, 4096),
        up_weight, up_bias.reshape(1, 512), down_weight,
    )
    outs = pl.pallas_call(
        hand_over,
        out_shape=tuple(shape(out.shape, out.dtype) for out in outs),
        in_specs=[vmem] * 6,
        out_specs=(vmem,) * 6,
    )(*outs)
    input_grad, up_grad, down_grad, up_bias_grad, gain_grad, bias_grad = outs
    return (
        input_grad, up_grad, down_grad, up_bias_grad.reshape(512), gain_grad.reshape(4096), bias_grad.reshape(4096),
    )


def solution(mesh):
    return jax.shard_map(
        shards,
        mesh=mesh,
        in_specs=(
            P(("tensor", "shard", "replica"), None),
            P(("tensor", "shard", "replica"), None),
            P(),
            P(),
            P("shard", "tensor"),
            P("tensor"),
            P("tensor", "shard"),
        ),
        out_specs=(
            P(("tensor", "shard", "replica"), None),
            P(("shard", "replica"), "tensor"),
            P("tensor", ("shard", "replica")),
            P("tensor"),
            P(),
            P(),
        ),
        check_vma=False,
    )
```

```python
import functools
import jax
import jax.numpy as jnp
from jax import lax
from jax.experimental import pallas as pl
from jax.experimental.pallas import tpu as pltpu
from jax.sharding import PartitionSpec as P

MESH = pl.DeviceIdType.MESH
NX, NY, NZ = 4, 4, 8


def when(cond, body):
    if cond is None:
        body()
    else:
        pl.when(cond)(body)


class Arrival:
    def __init__(self, copy, cond):
        self.copy, self.cond = copy, cond

    def wait_recv(self):
        when(self.cond, self.copy.wait_recv)

    def wait_send(self):
        when(self.cond, self.copy.wait_send)


class Links:
    def __init__(self, send, recv):
        self.send, self.recv, self.count, self.open = send, recv, 0, []

    def push(self, src, dst, landed, device, go=None, come=None):
        slot = self.count
        self.count += 1
        pair = dict(
            send_sem=self.send.at[slot], recv_sem=self.recv.at[slot], device_id=device, device_id_type=MESH
        )
        when(go, pltpu.make_async_remote_copy(src_ref=src, dst_ref=dst, **pair).start)
        arrival = pltpu.make_async_remote_copy(src_ref=src, dst_ref=landed, **pair)
        self.open.append(Arrival(arrival, go))
        return Arrival(arrival, come)

    def drain(self):
        for arrival in self.open:
            arrival.wait_send()
        self.open = []


def place():
    t, s, c = lax.axis_index("tensor"), lax.axis_index("shard"), lax.axis_index("replica")
    return t, s, c, s // NY, s % NY, t // NZ, t % NZ


def greet(devices):
    barrier = pltpu.get_barrier_semaphore()
    for device in devices:
        pl.semaphore_signal(barrier, inc=1, device_id=device, device_id_type=MESH)
    pl.semaphore_wait(barrier, len(devices))


def mm(left, right, dims):
    return lax.dot_general(left, right, (dims, ((), ())), preferred_element_type=jnp.float32)


def kernel(
    tok_in, grad_in, gain_hbm, nbias_hbm, up_in, ubias_hbm, down_in,
    dx_out, up_out, down_out, ub_out, gg_out, bg_out,
    A, XN, W, gain, nbias, ubias, raw, std, inv, mu, iv, act_t, lt, dh, acc, dacc,
    dxs, zr, rb, zsum, hin, dn16, dn, gz, gh, gsum, gb, gy, gx,
    P, CH, F, CE, DR, Y, YR, keep, ut, sums, local, send, recv,
):
    bf, f32 = jnp.bfloat16, jnp.float32
    t, s, c, x, yl, yh, z = place()
    sib = {"replica": 1 - c}
    xdev = lambda k: {"shard": ((x + k) % NX) * NY + yl}
    ydev = lambda k: {"shard": x * NY + (yl + k) % NY}
    zdev = lambda k: {"tensor": yh * NZ + (z + k) % NZ}
    opp = {"tensor": (1 - yh) * NZ + z}
    sof = lambda dx, dy: ((x + dx + NX) % NX) * NY + (yl + dy + NY) % NY
    tof = lambda dh, dz: ((yh + dh) % 2) * NZ + (z + dz + NZ) % NZ
    net = Links(send, recv)
    first_core, second_core = c == 0, c == 1

    def own_weights(act):
        for core, take in (
            (first_core, lambda h: up_in.at[:, pl.ds(h * 256, 256)]),
            (second_core, lambda h: down_in.at[pl.ds(h * 256, 256), :]),
        ):

            @pl.when(core)
            def _():
                for h in range(2):
                    act(pltpu.make_async_copy(take(h), W.at[s, h], local.at[h]))

    mine = [
        pltpu.make_async_copy(gain_hbm, gain, local.at[2]),
        pltpu.make_async_copy(nbias_hbm, nbias, local.at[3]),
        pltpu.make_async_copy(ubias_hbm, ubias, local.at[4]),
    ]
    own_weights(lambda copy: copy.start())
    for copy in mine:
        copy.start()
    raw[c, 0] = tok_in[...].astype(f32)
    raw[c, 1] = grad_in[...].astype(f32)
    greet([sib, opp] + [xdev(k) for k in (1, 2, 3)] + [ydev(k) for k in (1, 2, 3)] + [zdev(k) for k in range(1, NZ)])
    first = net.push(raw.at[c, 1 - c], raw.at[c, 1 - c], raw.at[1 - c, c], sib)
    own_weights(lambda copy: copy.wait())

    has_left, has_right = yl > 0, yl < NY - 1
    line, xin, far = {}, {}, {}

    def there(side, k):
        return yl - 1 - k >= 0 if side < 0 else yl + 1 + k <= NY - 1

    def along(side, k):
        here, landed = sof(0, side * k), sof(0, side * (k + 1))
        if side < 0:
            go = has_right if k == 0 else jnp.logical_and(has_right, yl - k >= 0)
        else:
            go = has_left if k == 0 else jnp.logical_and(has_left, yl + k <= NY - 1)
        line[side, k] = net.push(W.at[here], W.at[here], W.at[landed], ydev(1 if side < 0 else 3), go, there(side, k))

    def xsend(name, dy, cond):
        here, left, right = sof(0, dy), sof(-1, dy), sof(1, dy)
        xin[name] = [
            net.push(W.at[here, 0], W.at[here, 0], W.at[right, 0], xdev(3), cond, cond),
            net.push(W.at[here, 1], W.at[here, 1], W.at[left, 1], xdev(1), cond, cond),
            net.push(W.at[here, 0], W.at[here, 0], W.at[left, 0], xdev(1), cond, cond),
            net.push(W.at[here, 1], W.at[here, 1], W.at[right, 1], xdev(3), cond, cond),
        ]

    def xforward(name, dy, cond):
        left, right, opposite = sof(-1, dy), sof(1, dy), sof(2, dy)
        xin[name][0].wait_recv()
        one = net.push(W.at[right, 0], W.at[right, 0], W.at[opposite, 0], xdev(3), cond, cond)
        xin[name][1].wait_recv()
        two = net.push(W.at[left, 1], W.at[left, 1], W.at[opposite, 1], xdev(1), cond, cond)
        xin[name][2].wait_recv()
        xin[name][3].wait_recv()
        far[name] = (one, two)

    def yland(k):
        for side in (-1, 1):
            line[side, k].wait_recv()
            if k < 2:
                along(side, k + 1)
            xsend((side, k), side * (k + 1), there(side, k))

    def pass_x(k):
        for side in (-1, 1):
            xforward((side, k), side * (k + 1), there(side, k))

    along(-1, 0)
    along(1, 0)
    xsend("own", 0, None)

    ring = {}

    def part(slot, h):
        return A.at[slot, :, pl.ds(h * 2048, 2048)]

    def zsend(q, k, h):
        a, b = tof(q, -k), tof(q, k)
        right = net.push(part(a, h), part(a, h), part(tof(q, -k - 1), h), zdev(1)) if k < 3 or q == 0 else None
        left = net.push(part(b, h), part(b, h), part(tof(q, k + 1), h), zdev(7)) if k < 3 or q == 1 else None
        ring[q, k, h] = (right, left)

    def zland(q, k):
        for h in range(2):
            for arrival in ring[q, k, h]:
                if arrival is not None:
                    arrival.wait_recv()
            if k < 3:
                zsend(q, k + 1, h)

    def normalize(slot):
        @pl.when(first_core)
        def _():
            wide = A[slot].astype(f32)
            mean = jnp.mean(wide, axis=-1, keepdims=True)
            centred = wide - mean
            istd = lax.rsqrt(jnp.mean(centred * centred, axis=-1, keepdims=True) + 1e-05)
            XN[slot] = (centred * istd * gain[...] + nbias[...]).astype(bf)
            mu[slot] = jnp.broadcast_to(mean, (16, 128))
            iv[slot] = jnp.broadcast_to(istd, (16, 128))

        @pl.when(second_core)
        def _():
            XN[slot] = A[slot]

    def settle(k):
        if k == "y":
            normalize(tof(1, 0))
        elif k < 3:

            @pl.loop(0, 4)
            def _(i):
                normalize(((yh + i // 2) % 2) * NZ + (z + (2 * (i % 2) - 1) * (k + 1) + NZ) % NZ)
        else:

            @pl.loop(0, 2)
            def _(i):
                normalize(((yh + i) % 2) * NZ + (z + 4) % NZ)

    first.wait_recv()
    A[t] = jnp.concatenate([raw[0, c], raw[1, c]], axis=0).astype(bf)
    over = [net.push(part(t, h), part(t, h), part(tof(1, 0), h), opp) for h in range(2)]
    for h in range(2):
        zsend(0, 0, h)
    for copy in mine:
        copy.wait()
    normalize(t)
    yland(0)
    for h in range(2):
        over[h].wait_recv()
        zsend(1, 0, h)
    zland(0, 0)
    xforward("own", 0, None)
    zland(1, 0)
    yland(1)
    settle("y")
    zland(0, 1)
    pass_x(0)
    zland(1, 1)
    yland(2)
    settle(0)
    zland(0, 2)
    zland(1, 2)
    settle(1)
    pass_x(1)
    zland(0, 3)
    zland(1, 3)
    settle(2)
    wide = raw[c, 0]
    centred = wide - jnp.mean(wide, axis=-1, keepdims=True)
    istd = lax.rsqrt(jnp.mean(centred * centred, axis=-1, keepdims=True) + 1e-05)
    inv[...] = jnp.broadcast_to(istd, inv.shape)
    std[...] = centred * istd
    settle(3)

    def forward(s1):
        cols = pl.ds(pl.multiple_of(s1 * 256, 256), 256)
        for core, dims in ((first_core, ((1,), (0,))), (second_core, ((1,), (1,)))):

            @pl.when(core)
            def _():
                right = XN[:, :, cols].reshape(256, 256)
                for h in range(2):
                    acc[h] += mm(right, W[s1, h], dims)

    for h in range(2):
        start = jnp.where(first_core, ubias[:, h * 256 : (h + 1) * 256], 0.0)
        acc[h] = jnp.broadcast_to(start, (256, 256))
    remote = lambda y1: jnp.abs(y1 - yl) == 3
    near = lambda i, y1: ((x + i + i // 2) % NX) * NY + y1

    @pl.loop(0, 12)
    def _(i):
        @pl.when(jnp.logical_not(remote(i // 3)))
        def _():
            forward(near(i % 3, i // 3))

    pass_x(2)
    for name in ("own", (-1, 0), (1, 0), (-1, 1), (1, 1)):
        for arrival in far[name]:
            arrival.wait_recv()

    @pl.loop(0, 4)
    def _(y1):
        @pl.when(jnp.logical_not(remote(y1)))
        def _():
            forward(((x + 2) % NX) * NY + y1)

    ends_line = jnp.logical_or(yl == 0, yl == 3)

    @pl.when(ends_line)
    def _():
        @pl.loop(0, 3)
        def _(i):
            forward(near(i, 3 - yl))

    for name in ((-1, 2), (1, 2)):
        for arrival in far[name]:
            arrival.wait_recv()

    @pl.when(ends_line)
    def _():
        forward(((x + 2) % NX) * NY + 3 - yl)

    d_act_in = net.push(acc, dacc, dacc, sib, second_core, first_core)

    @pl.when(first_core)
    def _():
        root = 0.7978845608028654
        for h in range(2):
            v = acc[h]
            th = jnp.tanh(root * (v + 0.044715 * v * v * v))
            act_t[h] = jnp.transpose(0.5 * v * (1.0 + th)).astype(bf)
            acc[h] = 0.5 * (1.0 + th) + 0.5 * v * (1.0 - th * th) * (root * (1.0 + 3 * 0.044715 * v * v))

    act_in = net.push(act_t, lt, lt, sib, first_core, second_core)
    d_act_in.wait_recv()

    @pl.when(first_core)
    def _():
        gb[32:40, :] = jnp.zeros((8, 256), f32)
        for h in range(2):
            d_pre = (dacc[h] * acc[h]).astype(bf)
            dh[h] = d_pre
            lt[h] = jnp.transpose(d_pre.astype(f32)).astype(bf)
            gb[32 + h : 33 + h, :] = jnp.sum(d_pre.astype(f32), axis=0, keepdims=True)

    act_in.wait_recv()

    chain, direct, ends, ysums = {}, {}, {}, {}

    def partials(k):
        @pl.loop(0, 4)
        def _(i):
            s1 = i * NY + (yl + k) % NY
            cols = pl.ds(pl.multiple_of(s1 * 256, 256), 256)
            right = XN[:, :, cols].reshape(256, 256)
            for h in range(2):
                P[h, s1] = mm(lt[h], right, ((1,), (0,))).astype(bf)

        chain[k] = (
            net.push(P.at[0, sof(2, k)], CH.at[0, k], CH.at[0, k], xdev(3)),
            net.push(P.at[1, sof(2, k)], CH.at[1, k], CH.at[1, k], xdev(1)),
        )
        direct[k] = (
            net.push(P.at[0, sof(1, k)], DR.at[0, k], DR.at[0, k], xdev(1)),
            net.push(P.at[1, sof(-1, k)], DR.at[1, k], DR.at[1, k], xdev(3)),
        )

    def pass_on(k):
        for u, (dx, device) in enumerate(((-1, xdev(3)), (1, xdev(1)))):
            chain[k][u].wait_recv()
            F[u, k] = (CH[u, k].astype(f32) + P[u, sof(dx, k)].astype(f32)).astype(bf)
            ends[u, k] = net.push(F.at[u, k], CE.at[u, k], CE.at[u, k], device)

    def finish_x(k):
        for u in range(2):
            direct[k][u].wait_recv()
            ends[u, k].wait_recv()
            total = P[u, sof(0, k)].astype(f32) + CE[u, k].astype(f32) + DR[u, k].astype(f32)
            if k == 0:
                keep[u] = total
            else:
                Y[u, k] = total.astype(bf)
                ysums[u, k] = net.push(Y.at[u, k], YR.at[u, k], YR.at[u, k], ydev(k))

    def d_normed_part(j):
        @pl.when(first_core)
        def _():
            @pl.loop(0, 8)
            def _(i):
                block = j * 8 + i
                total = mm(dh[0], W[block, 0], ((1,), (1,))) + mm(dh[1], W[block, 1], ((1,), (1,)))
                dxs[j, :, :, pl.ds(pl.multiple_of(i * 256, 256), 256)] = total.astype(bf).reshape(16, 16, 256)
                tok = A[:, :, pl.ds(pl.multiple_of(block * 256, 256), 256)].reshape(256, 256).astype(f32)
                standard = (tok - mu[...].reshape(256, 128)[:, 0:1]) * iv[...].reshape(256, 128)[:, 0:1]
                gsum[pl.ds(block, 1), :] = jnp.sum(total * standard, axis=0, keepdims=True)
                gsum[pl.ds(16 + block, 1), :] = jnp.sum(total, axis=0, keepdims=True)

        def zpush(to, slot, device, h):
            return net.push(
                dxs.at[j, h * NZ + (z + to) % NZ], zr.at[slot, h, j], zr.at[slot, h, j], zdev(device), first_core, first_core
            )

        joins[j] = [zpush(4, 4, 2, 0), zpush(4, 4, 6, 1)]
        for h in range(2):
            joins[j] += [zpush(3, 3, 1, h), zpush(5, 5, 7, h)]
        for h in range(2):
            zin.extend([zpush(1, 1, 1, h), zpush(7, 7, 7, h)])

    def join(j):
        for arrival in joins[j]:
            arrival.wait_recv()

        @pl.when(first_core)
        def _():
            for d, (to, slot) in enumerate(((2, 3), (6, 5))):
                for h in range(2):
                    total = dxs[j, h * NZ + (z + to) % NZ].astype(f32) + zr[slot, h, j].astype(f32)
                    if h == d:
                        total += zr[4, h, j].astype(f32)
                    rb[d, h, j] = total.astype(bf)

        for d, to in enumerate((2, 6)):
            for h in range(2):
                zin.append(
                    net.push(rb.at[d, h, j], zr.at[to, h, j], zr.at[to, h, j], zdev(to), first_core, first_core)
                )

    joins = {}
    zin = []
    partials(2)
    d_normed_part(0)
    partials(1)
    d_normed_part(1)
    zg = [net.push(gsum, gz.at[k], gz.at[k], zdev(k), first_core, first_core) for k in range(1, NZ)]
    pass_on(2)
    join(0)
    partials(3)
    pass_on(1)
    join(1)
    finish_x(2)
    partials(0)
    for arrival in zg:
        arrival.wait_recv()

    @pl.when(first_core)
    def _():
        total = gsum[...]
        for k in range(1, NZ):
            total += gz[k]
        gb[0:32, :] = total

    hg = net.push(gb.at[0:32, :], gh, gh, opp, first_core, first_core)
    pass_on(3)
    finish_x(1)
    hg.wait_recv()

    @pl.when(first_core)
    def _():
        gy[0, 32:40, :] = gb[32:40, :]
        gy[0, 0:32, :] = gb[0:32, :] + gh[...]

    yg = [net.push(gy.at[0], gy.at[k], gy.at[k], ydev(k), first_core, first_core) for k in (1, 2, 3)]

    pass_on(0)
    for arrival in zin:
        arrival.wait_recv()

    def zadd(h, j):
        total = dxs[j, h * NZ + z].astype(f32)
        for k in (1, 7, 2, 6):
            total += zr[k, h, j].astype(f32)
        return total

    @pl.when(first_core)
    def _():
        for j in range(2):
            zsum[j] = zadd(1 - yh, j).astype(bf)

    over = net.push(zsum, hin, hin, opp, first_core, first_core)

    @pl.when(first_core)
    def _():
        for j in range(2):
            dn16[j] = zadd(yh, j)

    finish_x(3)
    for arrival in yg:
        arrival.wait_recv()

    @pl.when(first_core)
    def _():
        gx[0] = gy[0] + gy[1] + gy[2] + gy[3]

    xg = [net.push(gx.at[0], gx.at[k], gx.at[k], xdev(k), first_core, first_core) for k in (1, 2, 3)]
    over.wait_recv()

    @pl.when(first_core)
    def _():
        for j in range(2):
            dn16[j] += hin[j].astype(f32)
            dn[j] = dn16[j, 0:8, :]

    rows_out = net.push(dn16.at[:, 8:16, :], dn, dn, sib, first_core, second_core)
    for arrival in xg:
        arrival.wait_recv()

    @pl.when(first_core)
    def _():
        sums[...] = gx[0] + gx[1] + gx[2] + gx[3]

    last = [net.push(sums, sums, sums, sib, first_core, second_core)]
    rows_out.wait_recv()
    d_normed = jnp.concatenate([dn[0], dn[1]], axis=1)
    scaled = d_normed * gain[...]
    mean1 = jnp.mean(scaled, axis=-1, keepdims=True)
    mean2 = jnp.mean(scaled * std[...], axis=-1, keepdims=True)
    d_in = inv[:, 0:1] * (scaled - mean1 - std[...] * mean2)
    dx_out[...] = (raw[c, 1] + d_in).astype(bf)
    finish_x(0)
    for u in range(2):
        total = keep[u]
        for k in (1, 2, 3):
            ysums[u, k].wait_recv()
            total += YR[u, k].astype(f32)

        @pl.when(first_core)
        def _():
            ut[u] = jnp.transpose(total)

        @pl.when(second_core)
        def _():
            ut[u] = total

    def own_grads(act):
        @pl.when(first_core)
        def _():
            for h in range(2):
                act(pltpu.make_async_copy(ut.at[h, 0:128, :], up_out.at[:, pl.ds(h * 256, 256)], local.at[h]))

        @pl.when(second_core)
        def _():
            for h in range(2):
                act(pltpu.make_async_copy(ut.at[h, :, 128:256], down_out.at[pl.ds(h * 256, 256), :], local.at[h]))

    for h in range(2):
        up_part, down_part = up_out.at[:, pl.ds(h * 256, 256)], down_out.at[pl.ds(h * 256, 256), :]
        last.append(net.push(ut.at[h, 128:256, :], up_part, up_part, sib, first_core, second_core))
        last.append(net.push(ut.at[h, :, 0:128], down_part, down_part, sib, second_core, first_core))
    own_grads(lambda copy: copy.start())
    last[0].wait_recv()
    for h in range(2):
        ub_out[:, h * 256 : (h + 1) * 256] = sums[32 + h : 33 + h, :]
    for i in range(16):
        cols = slice(i * 256, (i + 1) * 256)
        gg_out[:, cols] = sums[i : i + 1, :]
        bg_out[:, cols] = sums[16 + i : 17 + i, :]
    for arrival in last[1:]:
        arrival.wait_recv()
    own_grads(lambda copy: copy.wait())
    net.drain()


def hand_over(*refs):
    for source, result in zip(refs[:6], refs[6:]):
        result[...] = source[...]


def shards(tokens, grad_out, norm_gain, norm_bias, up_weight, up_bias, down_weight):
    vmem, hbm = pl.BlockSpec(memory_space=pltpu.VMEM), pl.BlockSpec(memory_space=pltpu.HBM)
    bf, f32 = jnp.bfloat16, jnp.float32
    shape, room = jax.ShapeDtypeStruct, pltpu.VMEM
    outs = pl.pallas_call(
        kernel,
        out_shape=(
            shape((8, 4096), bf), shape((128, 512), f32), shape((512, 128), f32),
            shape((1, 512), f32), shape((1, 4096), f32), shape((1, 4096), f32),
        ),
        in_specs=[vmem, vmem, hbm, hbm, hbm, hbm, hbm],
        out_specs=(vmem,) * 6,
        scratch_shapes=[
            room((16, 16, 4096), bf),
            room((16, 16, 4096), bf),
            room((16, 2, 256, 256), bf),
            room((1, 4096), f32),
            room((1, 4096), f32),
            room((1, 512), f32),
            room((2, 2, 8, 4096), f32),
            room((8, 4096), f32),
            room((8, 128), f32),
            room((16, 16, 128), f32),
            room((16, 16, 128), f32),
            room((2, 256, 256), bf),
            room((2, 256, 256), bf),
            room((2, 256, 256), bf),
            room((2, 256, 256), f32),
            room((2, 256, 256), f32),
            room((2, 16, 16, 2048), bf),
            room((8, 2, 2, 16, 2048), bf),
            room((2, 2, 2, 16, 2048), bf),
            room((2, 16, 2048), bf),
            room((2, 16, 2048), bf),
            room((2, 16, 2048), f32),
            room((2, 8, 2048), f32),
            room((8, 32, 256), f32),
            room((32, 256), f32),
            room((32, 256), f32),
            room((40, 256), f32),
            room((4, 40, 256), f32),
            room((4, 40, 256), f32),
            room((2, 16, 256, 256), bf),
            room((2, 4, 256, 256), bf),
            room((2, 4, 256, 256), bf),
            room((2, 4, 256, 256), bf),
            room((2, 4, 256, 256), bf),
            room((2, 4, 256, 256), bf),
            room((2, 4, 256, 256), bf),
            room((2, 256, 256), f32),
            room((2, 256, 256), f32),
            room((40, 256), f32),
            pltpu.SemaphoreType.DMA((5,)),
            pltpu.SemaphoreType.DMA((220,)),
            pltpu.SemaphoreType.DMA((220,)),
        ],
        compiler_params=pltpu.CompilerParams(
            collective_id=0, has_side_effects=True, vmem_limit_bytes=63 << 20
        ),
    )(
        tokens, grad_out, norm_gain.reshape(1, 4096), norm_bias.reshape(1, 4096),
        up_weight, up_bias.reshape(1, 512), down_weight,
    )
    outs = pl.pallas_call(
        hand_over,
        out_shape=tuple(shape(out.shape, out.dtype) for out in outs),
        in_specs=[vmem] * 6,
        out_specs=(vmem,) * 6,
    )(*outs)
    input_grad, up_grad, down_grad, up_bias_grad, gain_grad, bias_grad = outs
    return (
        input_grad, up_grad, down_grad, up_bias_grad.reshape(512), gain_grad.reshape(4096), bias_grad.reshape(4096),
    )


def solution(mesh):
    return jax.shard_map(
        shards,
        mesh=mesh,
        in_specs=(
            P(("tensor", "shard", "replica"), None),
            P(("tensor", "shard", "replica"), None),
            P(),
            P(),
            P("shard", "tensor"),
            P("tensor"),
            P("tensor", "shard"),
        ),
        out_specs=(
            P(("tensor", "shard", "replica"), None),
            P(("shard", "replica"), "tensor"),
            P("tensor", ("shard", "replica")),
            P("tensor"),
            P(),
            P(),
        ),
        check_vma=False,
    )
```

```python
import functools
import jax
import jax.numpy as jnp
from jax import lax
from jax.experimental import pallas as pl
from jax.experimental.pallas import tpu as pltpu
from jax.sharding import PartitionSpec as P

MESH = pl.DeviceIdType.MESH
NX, NY, NZ = 4, 4, 8


def when(cond, body):
    if cond is None:
        body()
    else:
        pl.when(cond)(body)


class Arrival:
    def __init__(self, copy, cond):
        self.copy, self.cond = copy, cond

    def wait_recv(self):
        when(self.cond, self.copy.wait_recv)

    def wait_send(self):
        when(self.cond, self.copy.wait_send)


class Links:
    def __init__(self, send, recv):
        self.send, self.recv, self.count, self.open = send, recv, 0, []

    def push(self, src, dst, landed, device, go=None, come=None):
        slot = self.count
        self.count += 1
        pair = dict(
            send_sem=self.send.at[slot], recv_sem=self.recv.at[slot], device_id=device, device_id_type=MESH
        )
        when(go, pltpu.make_async_remote_copy(src_ref=src, dst_ref=dst, **pair).start)
        arrival = pltpu.make_async_remote_copy(src_ref=src, dst_ref=landed, **pair)
        self.open.append(Arrival(arrival, go))
        return Arrival(arrival, come)

    def drain(self):
        for arrival in self.open:
            arrival.wait_send()
        self.open = []


def place():
    t, s, c = lax.axis_index("tensor"), lax.axis_index("shard"), lax.axis_index("replica")
    return t, s, c, s // NY, s % NY, t // NZ, t % NZ


def greet(devices):
    barrier = pltpu.get_barrier_semaphore()
    for device in devices:
        pl.semaphore_signal(barrier, inc=1, device_id=device, device_id_type=MESH)
    pl.semaphore_wait(barrier, len(devices))


def mm(left, right, dims):
    return lax.dot_general(left, right, (dims, ((), ())), preferred_element_type=jnp.float32)


def kernel(
    tok_in, grad_in, gain_hbm, nbias_hbm, up_in, ubias_hbm, down_in,
    dx_out, up_out, down_out, ub_out, gg_out, bg_out,
    A, XN, W, gain, nbias, ubias, raw, std, inv, mu, iv, act_t, lt, dh, acc, dacc,
    dxs, zr, rb, zsum, hin, dn16, dn, gz, gh, gsum, gb, gy, gx,
    P, CH, F, CE, DR, Y, YR, keep, ut, sums, local, send, recv,
):
    bf, f32 = jnp.bfloat16, jnp.float32
    t, s, c, x, yl, yh, z = place()
    sib = {"replica": 1 - c}
    xdev = lambda k: {"shard": ((x + k) % NX) * NY + yl}
    ydev = lambda k: {"shard": x * NY + (yl + k) % NY}
    zdev = lambda k: {"tensor": yh * NZ + (z + k) % NZ}
    opp = {"tensor": (1 - yh) * NZ + z}
    sof = lambda dx, dy: ((x + dx + NX) % NX) * NY + (yl + dy + NY) % NY
    tof = lambda dh, dz: ((yh + dh) % 2) * NZ + (z + dz + NZ) % NZ
    net = Links(send, recv)
    first_core, second_core = c == 0, c == 1

    def own_weights(act):
        for core, take in (
            (first_core, lambda h: up_in.at[:, pl.ds(h * 256, 256)]),
            (second_core, lambda h: down_in.at[pl.ds(h * 256, 256), :]),
        ):

            @pl.when(core)
            def _():
                for h in range(2):
                    act(pltpu.make_async_copy(take(h), W.at[s, h], local.at[h]))

    mine = [
        pltpu.make_async_copy(gain_hbm, gain, local.at[2]),
        pltpu.make_async_copy(nbias_hbm, nbias, local.at[3]),
        pltpu.make_async_copy(ubias_hbm, ubias, local.at[4]),
    ]
    own_weights(lambda copy: copy.start())
    for copy in mine:
        copy.start()
    raw[c, 0] = tok_in[...].astype(f32)
    raw[c, 1] = grad_in[...].astype(f32)
    greet([sib, opp] + [xdev(k) for k in (1, 2, 3)] + [ydev(k) for k in (1, 2, 3)] + [zdev(k) for k in range(1, NZ)])
    first = net.push(raw.at[c, 1 - c], raw.at[c, 1 - c], raw.at[1 - c, c], sib)
    own_weights(lambda copy: copy.wait())

    has_left, has_right = yl > 0, yl < NY - 1
    line, xin, far = {}, {}, {}

    def there(side, k):
        return yl - 1 - k >= 0 if side < 0 else yl + 1 + k <= NY - 1

    def along(side, k):
        here, landed = sof(0, side * k), sof(0, side * (k + 1))
        if side < 0:
            go = has_right if k == 0 else jnp.logical_and(has_right, yl - k >= 0)
        else:
            go = has_left if k == 0 else jnp.logical_and(has_left, yl + k <= NY - 1)
        line[side, k] = net.push(W.at[here], W.at[here], W.at[landed], ydev(1 if side < 0 else 3), go, there(side, k))

    def xsend(name, dy, cond):
        here, left, right = sof(0, dy), sof(-1, dy), sof(1, dy)
        xin[name] = [
            net.push(W.at[here], W.at[here], W.at[right], xdev(3), cond, cond),
            net.push(W.at[here], W.at[here], W.at[left], xdev(1), cond, cond),
        ]

    def xforward(name, dy, cond):
        left, right, opposite = sof(-1, dy), sof(1, dy), sof(2, dy)
        xin[name][0].wait_recv()
        one = net.push(W.at[right, 0], W.at[right, 0], W.at[opposite, 0], xdev(3), cond, cond)
        xin[name][1].wait_recv()
        two = net.push(W.at[left, 1], W.at[left, 1], W.at[opposite, 1], xdev(1), cond, cond)
        far[name] = (one, two)

    def yland(k):
        for side in (-1, 1):
            line[side, k].wait_recv()
            if k < 2:
                along(side, k + 1)
            xsend((side, k), side * (k + 1), there(side, k))

    def pass_x(k):
        for side in (-1, 1):
            xforward((side, k), side * (k + 1), there(side, k))

    along(-1, 0)
    along(1, 0)
    xsend("own", 0, None)

    ring = {}

    def part(slot, h):
        return A.at[slot, :, pl.ds(h * 2048, 2048)]

    def zsend(q, k, h):
        a, b = tof(q, -k), tof(q, k)
        right = net.push(part(a, h), part(a, h), part(tof(q, -k - 1), h), zdev(1)) if k < 3 or q == 0 else None
        left = net.push(part(b, h), part(b, h), part(tof(q, k + 1), h), zdev(7)) if k < 3 or q == 1 else None
        ring[q, k, h] = (right, left)

    def zland(q, k):
        for h in range(2):
            for arrival in ring[q, k, h]:
                if arrival is not None:
                    arrival.wait_recv()
            if k < 3:
                zsend(q, k + 1, h)

    def normalize(slot):
        @pl.when(first_core)
        def _():
            wide = A[slot].astype(f32)
            mean = jnp.mean(wide, axis=-1, keepdims=True)
            centred = wide - mean
            istd = lax.rsqrt(jnp.mean(centred * centred, axis=-1, keepdims=True) + 1e-05)
            XN[slot] = (centred * istd * gain[...] + nbias[...]).astype(bf)
            mu[slot] = jnp.broadcast_to(mean, (16, 128))
            iv[slot] = jnp.broadcast_to(istd, (16, 128))

        @pl.when(second_core)
        def _():
            XN[slot] = A[slot]

    def settle(k):
        if k == "y":
            normalize(tof(1, 0))
        elif k < 3:

            @pl.loop(0, 4)
            def _(i):
                normalize(((yh + i // 2) % 2) * NZ + (z + (2 * (i % 2) - 1) * (k + 1) + NZ) % NZ)
        else:

            @pl.loop(0, 2)
            def _(i):
                normalize(((yh + i) % 2) * NZ + (z + 4) % NZ)

    first.wait_recv()
    A[t] = jnp.concatenate([raw[0, c], raw[1, c]], axis=0).astype(bf)
    over = [net.push(part(t, h), part(t, h), part(tof(1, 0), h), opp) for h in range(2)]
    for h in range(2):
        zsend(0, 0, h)
    for copy in mine:
        copy.wait()
    normalize(t)
    yland(0)
    for h in range(2):
        over[h].wait_recv()
        zsend(1, 0, h)
    zland(0, 0)
    xforward("own", 0, None)
    zland(1, 0)
    yland(1)
    settle("y")
    zland(0, 1)
    pass_x(0)
    zland(1, 1)
    yland(2)
    settle(0)
    zland(0, 2)
    zland(1, 2)
    settle(1)
    pass_x(1)
    zland(0, 3)
    zland(1, 3)
    settle(2)
    wide = raw[c, 0]
    centred = wide - jnp.mean(wide, axis=-1, keepdims=True)
    istd = lax.rsqrt(jnp.mean(centred * centred, axis=-1, keepdims=True) + 1e-05)
    inv[...] = jnp.broadcast_to(istd, inv.shape)
    std[...] = centred * istd
    settle(3)

    def forward(s1):
        cols = pl.ds(pl.multiple_of(s1 * 256, 256), 256)
        for core, dims in ((first_core, ((1,), (0,))), (second_core, ((1,), (1,)))):

            @pl.when(core)
            def _():
                right = XN[:, :, cols].reshape(256, 256)
                for h in range(2):
                    acc[h] += mm(right, W[s1, h], dims)

    for h in range(2):
        start = jnp.where(first_core, ubias[:, h * 256 : (h + 1) * 256], 0.0)
        acc[h] = jnp.broadcast_to(start, (256, 256))
    remote = lambda y1: jnp.abs(y1 - yl) == 3
    near = lambda i, y1: ((x + i + i // 2) % NX) * NY + y1

    @pl.loop(0, 12)
    def _(i):
        @pl.when(jnp.logical_not(remote(i // 3)))
        def _():
            forward(near(i % 3, i // 3))

    pass_x(2)
    for name in ("own", (-1, 0), (1, 0), (-1, 1), (1, 1)):
        for arrival in far[name]:
            arrival.wait_recv()

    @pl.loop(0, 4)
    def _(y1):
        @pl.when(jnp.logical_not(remote(y1)))
        def _():
            forward(((x + 2) % NX) * NY + y1)

    ends_line = jnp.logical_or(yl == 0, yl == 3)

    @pl.when(ends_line)
    def _():
        @pl.loop(0, 3)
        def _(i):
            forward(near(i, 3 - yl))

    for name in ((-1, 2), (1, 2)):
        for arrival in far[name]:
            arrival.wait_recv()

    @pl.when(ends_line)
    def _():
        forward(((x + 2) % NX) * NY + 3 - yl)

    d_act_in = net.push(acc, dacc, dacc, sib, second_core, first_core)

    @pl.when(first_core)
    def _():
        root = 0.7978845608028654
        for h in range(2):
            v = acc[h]
            th = jnp.tanh(root * (v + 0.044715 * v * v * v))
            act_t[h] = jnp.transpose(0.5 * v * (1.0 + th)).astype(bf)
            acc[h] = 0.5 * (1.0 + th) + 0.5 * v * (1.0 - th * th) * (root * (1.0 + 3 * 0.044715 * v * v))

    act_in = net.push(act_t, lt, lt, sib, first_core, second_core)
    d_act_in.wait_recv()

    @pl.when(first_core)
    def _():
        gb[32:40, :] = jnp.zeros((8, 256), f32)
        for h in range(2):
            d_pre = (dacc[h] * acc[h]).astype(bf)
            dh[h] = d_pre
            lt[h] = jnp.transpose(d_pre.astype(f32)).astype(bf)
            gb[32 + h : 33 + h, :] = jnp.sum(d_pre.astype(f32), axis=0, keepdims=True)

    act_in.wait_recv()

    chain, direct, ends, ysums = {}, {}, {}, {}

    def partials(k):
        @pl.loop(0, 4)
        def _(i):
            s1 = i * NY + (yl + k) % NY
            cols = pl.ds(pl.multiple_of(s1 * 256, 256), 256)
            right = XN[:, :, cols].reshape(256, 256)
            for h in range(2):
                P[h, s1] = mm(lt[h], right, ((1,), (0,))).astype(bf)

        chain[k] = (
            net.push(P.at[0, sof(2, k)], CH.at[0, k], CH.at[0, k], xdev(3)),
            net.push(P.at[1, sof(2, k)], CH.at[1, k], CH.at[1, k], xdev(1)),
        )
        direct[k] = (
            net.push(P.at[0, sof(1, k)], DR.at[0, k], DR.at[0, k], xdev(1)),
            net.push(P.at[1, sof(-1, k)], DR.at[1, k], DR.at[1, k], xdev(3)),
        )

    def pass_on(k):
        for u, (dx, device) in enumerate(((-1, xdev(3)), (1, xdev(1)))):
            chain[k][u].wait_recv()
            F[u, k] = (CH[u, k].astype(f32) + P[u, sof(dx, k)].astype(f32)).astype(bf)
            ends[u, k] = net.push(F.at[u, k], CE.at[u, k], CE.at[u, k], device)

    def finish_x(k):
        for u in range(2):
            direct[k][u].wait_recv()
            ends[u, k].wait_recv()
            total = P[u, sof(0, k)].astype(f32) + CE[u, k].astype(f32) + DR[u, k].astype(f32)
            if k == 0:
                keep[u] = total
            else:
                Y[u, k] = total.astype(bf)
                ysums[u, k] = net.push(Y.at[u, k], YR.at[u, k], YR.at[u, k], ydev(k))

    def d_normed_part(j):
        @pl.when(first_core)
        def _():
            @pl.loop(0, 8)
            def _(i):
                block = j * 8 + i
                total = mm(dh[0], W[block, 0], ((1,), (1,))) + mm(dh[1], W[block, 1], ((1,), (1,)))
                dxs[j, :, :, pl.ds(pl.multiple_of(i * 256, 256), 256)] = total.astype(bf).reshape(16, 16, 256)
                tok = A[:, :, pl.ds(pl.multiple_of(block * 256, 256), 256)].reshape(256, 256).astype(f32)
                standard = (tok - mu[...].reshape(256, 128)[:, 0:1]) * iv[...].reshape(256, 128)[:, 0:1]
                gsum[pl.ds(block, 1), :] = jnp.sum(total * standard, axis=0, keepdims=True)
                gsum[pl.ds(16 + block, 1), :] = jnp.sum(total, axis=0, keepdims=True)

        def zpush(to, slot, device, h):
            return net.push(
                dxs.at[j, h * NZ + (z + to) % NZ], zr.at[slot, h, j], zr.at[slot, h, j], zdev(device), first_core, first_core
            )

        joins[j] = [zpush(4, 4, 2, 0), zpush(4, 4, 6, 1)]
        for h in range(2):
            joins[j] += [zpush(3, 3, 1, h), zpush(5, 5, 7, h)]
        for h in range(2):
            zin.extend([zpush(1, 1, 1, h), zpush(7, 7, 7, h)])

    def join(j):
        for arrival in joins[j]:
            arrival.wait_recv()

        @pl.when(first_core)
        def _():
            for d, (to, slot) in enumerate(((2, 3), (6, 5))):
                for h in range(2):
                    total = dxs[j, h * NZ + (z + to) % NZ].astype(f32) + zr[slot, h, j].astype(f32)
                    if h == d:
                        total += zr[4, h, j].astype(f32)
                    rb[d, h, j] = total.astype(bf)

        for d, to in enumerate((2, 6)):
            for h in range(2):
                zin.append(
                    net.push(rb.at[d, h, j], zr.at[to, h, j], zr.at[to, h, j], zdev(to), first_core, first_core)
                )

    joins = {}
    zin = []
    d_normed_part(0)
    partials(2)
    d_normed_part(1)
    partials(1)
    zg = [net.push(gsum, gz.at[k], gz.at[k], zdev(k), first_core, first_core) for k in range(1, NZ)]
    pass_on(2)
    join(0)
    partials(3)
    pass_on(1)
    join(1)
    finish_x(2)
    partials(0)
    for arrival in zg:
        arrival.wait_recv()

    @pl.when(first_core)
    def _():
        total = gsum[...]
        for k in range(1, NZ):
            total += gz[k]
        gb[0:32, :] = total

    hg = net.push(gb.at[0:32, :], gh, gh, opp, first_core, first_core)
    pass_on(3)
    finish_x(1)
    hg.wait_recv()

    @pl.when(first_core)
    def _():
        gy[0, 32:40, :] = gb[32:40, :]
        gy[0, 0:32, :] = gb[0:32, :] + gh[...]

    yg = [net.push(gy.at[0], gy.at[k], gy.at[k], ydev(k), first_core, first_core) for k in (1, 2, 3)]

    pass_on(0)
    for arrival in zin:
        arrival.wait_recv()

    def zadd(h, j):
        total = dxs[j, h * NZ + z].astype(f32)
        for k in (1, 7, 2, 6):
            total += zr[k, h, j].astype(f32)
        return total

    @pl.when(first_core)
    def _():
        for j in range(2):
            zsum[j] = zadd(1 - yh, j).astype(bf)

    over = net.push(zsum, hin, hin, opp, first_core, first_core)

    @pl.when(first_core)
    def _():
        for j in range(2):
            dn16[j] = zadd(yh, j)

    finish_x(3)
    for arrival in yg:
        arrival.wait_recv()

    @pl.when(first_core)
    def _():
        gx[0] = gy[0] + gy[1] + gy[2] + gy[3]

    xg = [net.push(gx.at[0], gx.at[k], gx.at[k], xdev(k), first_core, first_core) for k in (1, 2, 3)]
    over.wait_recv()

    @pl.when(first_core)
    def _():
        for j in range(2):
            dn16[j] += hin[j].astype(f32)
            dn[j] = dn16[j, 0:8, :]

    rows_out = net.push(dn16.at[:, 8:16, :], dn, dn, sib, first_core, second_core)
    for arrival in xg:
        arrival.wait_recv()

    @pl.when(first_core)
    def _():
        sums[...] = gx[0] + gx[1] + gx[2] + gx[3]

    last = [net.push(sums, sums, sums, sib, first_core, second_core)]
    rows_out.wait_recv()
    d_normed = jnp.concatenate([dn[0], dn[1]], axis=1)
    scaled = d_normed * gain[...]
    mean1 = jnp.mean(scaled, axis=-1, keepdims=True)
    mean2 = jnp.mean(scaled * std[...], axis=-1, keepdims=True)
    d_in = inv[:, 0:1] * (scaled - mean1 - std[...] * mean2)
    dx_out[...] = (raw[c, 1] + d_in).astype(bf)
    finish_x(0)
    for u in range(2):
        total = keep[u]
        for k in (1, 2, 3):
            ysums[u, k].wait_recv()
            total += YR[u, k].astype(f32)

        @pl.when(first_core)
        def _():
            ut[u] = jnp.transpose(total)

        @pl.when(second_core)
        def _():
            ut[u] = total

    def own_grads(act):
        @pl.when(first_core)
        def _():
            for h in range(2):
                act(pltpu.make_async_copy(ut.at[h, 0:128, :], up_out.at[:, pl.ds(h * 256, 256)], local.at[h]))

        @pl.when(second_core)
        def _():
            for h in range(2):
                act(pltpu.make_async_copy(ut.at[h, :, 128:256], down_out.at[pl.ds(h * 256, 256), :], local.at[h]))

    for h in range(2):
        up_part, down_part = up_out.at[:, pl.ds(h * 256, 256)], down_out.at[pl.ds(h * 256, 256), :]
        last.append(net.push(ut.at[h, 128:256, :], up_part, up_part, sib, first_core, second_core))
        last.append(net.push(ut.at[h, :, 0:128], down_part, down_part, sib, second_core, first_core))
    own_grads(lambda copy: copy.start())
    last[0].wait_recv()
    for h in range(2):
        ub_out[:, h * 256 : (h + 1) * 256] = sums[32 + h : 33 + h, :]
    for i in range(16):
        cols = slice(i * 256, (i + 1) * 256)
        gg_out[:, cols] = sums[i : i + 1, :]
        bg_out[:, cols] = sums[16 + i : 17 + i, :]
    for arrival in last[1:]:
        arrival.wait_recv()
    own_grads(lambda copy: copy.wait())
    net.drain()


def hand_over(*refs):
    for source, result in zip(refs[:6], refs[6:]):
        result[...] = source[...]


def shards(tokens, grad_out, norm_gain, norm_bias, up_weight, up_bias, down_weight):
    vmem, hbm = pl.BlockSpec(memory_space=pltpu.VMEM), pl.BlockSpec(memory_space=pltpu.HBM)
    bf, f32 = jnp.bfloat16, jnp.float32
    shape, room = jax.ShapeDtypeStruct, pltpu.VMEM
    outs = pl.pallas_call(
        kernel,
        out_shape=(
            shape((8, 4096), bf), shape((128, 512), f32), shape((512, 128), f32),
            shape((1, 512), f32), shape((1, 4096), f32), shape((1, 4096), f32),
        ),
        in_specs=[vmem, vmem, hbm, hbm, hbm, hbm, hbm],
        out_specs=(vmem,) * 6,
        scratch_shapes=[
            room((16, 16, 4096), bf),
            room((16, 16, 4096), bf),
            room((16, 2, 256, 256), bf),
            room((1, 4096), f32),
            room((1, 4096), f32),
            room((1, 512), f32),
            room((2, 2, 8, 4096), f32),
            room((8, 4096), f32),
            room((8, 128), f32),
            room((16, 16, 128), f32),
            room((16, 16, 128), f32),
            room((2, 256, 256), bf),
            room((2, 256, 256), bf),
            room((2, 256, 256), bf),
            room((2, 256, 256), f32),
            room((2, 256, 256), f32),
            room((2, 16, 16, 2048), bf),
            room((8, 2, 2, 16, 2048), bf),
            room((2, 2, 2, 16, 2048), bf),
            room((2, 16, 2048), bf),
            room((2, 16, 2048), bf),
            room((2, 16, 2048), f32),
            room((2, 8, 2048), f32),
            room((8, 32, 256), f32),
            room((32, 256), f32),
            room((32, 256), f32),
            room((40, 256), f32),
            room((4, 40, 256), f32),
            room((4, 40, 256), f32),
            room((2, 16, 256, 256), bf),
            room((2, 4, 256, 256), bf),
            room((2, 4, 256, 256), bf),
            room((2, 4, 256, 256), bf),
            room((2, 4, 256, 256), bf),
            room((2, 4, 256, 256), bf),
            room((2, 4, 256, 256), bf),
            room((2, 256, 256), f32),
            room((2, 256, 256), f32),
            room((40, 256), f32),
            pltpu.SemaphoreType.DMA((5,)),
            pltpu.SemaphoreType.DMA((220,)),
            pltpu.SemaphoreType.DMA((220,)),
        ],
        compiler_params=pltpu.CompilerParams(
            collective_id=0, has_side_effects=True, vmem_limit_bytes=63 << 20
        ),
    )(
        tokens, grad_out, norm_gain.reshape(1, 4096), norm_bias.reshape(1, 4096),
        up_weight, up_bias.reshape(1, 512), down_weight,
    )
    outs = pl.pallas_call(
        hand_over,
        out_shape=tuple(shape(out.shape, out.dtype) for out in outs),
        in_specs=[vmem] * 6,
        out_specs=(vmem,) * 6,
    )(*outs)
    input_grad, up_grad, down_grad, up_bias_grad, gain_grad, bias_grad = outs
    return (
        input_grad, up_grad, down_grad, up_bias_grad.reshape(512), gain_grad.reshape(4096), bias_grad.reshape(4096),
    )


def solution(mesh):
    return jax.shard_map(
        shards,
        mesh=mesh,
        in_specs=(
            P(("tensor", "shard", "replica"), None),
            P(("tensor", "shard", "replica"), None),
            P(),
            P(),
            P("shard", "tensor"),
            P("tensor"),
            P("tensor", "shard"),
        ),
        out_specs=(
            P(("tensor", "shard", "replica"), None),
            P(("shard", "replica"), "tensor"),
            P("tensor", ("shard", "replica")),
            P("tensor"),
            P(),
            P(),
        ),
        check_vma=False,
    )
```
